32 devices in a mesh: runs: 2 (over y), hst: 2 (over core), dom: 8 (over z, x).
Axes of the slice: x: 2, y: 2, z: 4, core: 2. Of those that a mesh axis runs over, the one named last changes fastest.
Arguments:
- features: bfloat16 [49152, 256], P(('runs', 'hst', 'dom')), parts along dimension 0, may hold values from -6 to 6
- aggregated: bfloat16 [49152, 256], P(('runs', 'hst', 'dom')), parts along dimension 0, may hold values from -6 to 6
- cotangent: bfloat16 [49152, 256], P(('runs', 'hst', 'dom')), parts along dimension 0, may hold values from -6 to 6
- w_self: bfloat16 [256, 256], replicated, may hold values from -0.375 to 0.375
- w_neigh: bfloat16 [256, 256], replicated, may hold values from -0.375 to 0.375
- tile_values: bfloat16 [32, 48, 128, 128], P(('runs', 'hst', 'dom')), parts along dimension 0, may hold values from -0.25 to 0.25
- tile_source: int32 [32, 48], P(('runs', 'hst', 'dom')), parts along dimension 0, may hold values from 0 to 11, as said below
- slot_source: int32 [32, 8, 8, 4], P(('runs', 'hst', 'dom')), parts along dimension 0, may hold values from 0 to 1535
- slot_weight: float32 [32, 8, 8, 4], P(('runs', 'hst', 'dom')), parts along dimension 0, may hold values from 0.25 to 1
- send_count: int32 [32, 8], P(('runs', 'hst', 'dom')), parts along dimension 0, may hold values from 0 to 8, as said below
- recv_rows: int32 [32, 8, 8], P(('runs', 'hst', 'dom')), parts along dimension 0, may hold values from 0 to 1535
- stale_grad: bfloat16 [32, 2, 64, 256], P(('runs', 'hst', 'dom')), parts along dimension 0, may hold values from -6 to 6
- version: int32 [32], P(('runs', 'hst', 'dom')), parts along dimension 0, may hold values from 0 to 1
- cross_source: int32 [32, 64, 4], P(('runs', 'hst', 'dom')), parts along dimension 0, may hold values from 0 to 63
- cross_weight: float32 [32, 64, 4], P(('runs', 'hst', 'dom')), parts along dimension 0, may hold values from 0.25 to 1
- cross_count: int32 [32], P(('runs', 'hst', 'dom')), parts along dimension 0, may hold values from 1 to 64, as said below
- cross_rows: int32 [32, 64], P(('runs', 'hst', 'dom')), parts along dimension 0, may hold values from 0 to 1535
Outputs:
- input_grad: bfloat16 [49152, 256], P(('runs', 'hst', 'dom')), parts along dimension 0
- weight_grads: bfloat16 [4, 256, 256], P('runs'), parts along dimension 0
The draws below stay inside these ranges and needn't reach their ends.
There are 2 independent parts, one for each index of `runs`. The reference program is written for one: setup_inputs(seed, part) draws one part's arguments, and reference() takes and returns one part's arrays. A program takes and returns all parts, laid end to end along the dimension named above; an argument that names none is the same for every part. Nothing has to cross between parts.
Inputs may be any that keep to these rules, and one draw needn't show every extreme that they name: `tile_source`: the 4 tiles of one destination block name different source blocks. Slots from index send_count on are padding. A device's own partition gets 0, and every device sends 8 to some other partition. Slots from index cross_count on are padding; some device has 64.
All inputs are finite; a program needn't handle non-finite values.
Results may differ from the reference program's by a relative error of at most 0.0054.
Values may be sent and summed in bfloat16 or wider, within the bound.
No kernel may reach another device: no remote copies, remote signals or barrier semaphores. Data moves between devices by JAX's collectives and lax.ppermute only.
A program may use at most 64 MiB of HBM per device.

```python
import math
import jax
import jax.numpy as jnp
from jax import lax

D = 256
ROWS = 1536
TPB = 4
CAP = 8
K = 4
XR = 64
XS = 64
PEERS = 8
DEVS = 16
NODES = 24576
LT = 48
N_HST = 2


def draw_tile_source(key, part):
    key = jax.random.fold_in(key, 7)
    subkeys = jax.random.split(key, DEVS * (ROWS // 128))
    picks = jax.vmap(lambda single: jax.random.permutation(single, ROWS // 128)[:TPB])(subkeys)
    return picks.reshape(DEVS, LT).astype(jnp.int32)


def draw_send_count(key, part):
    key = jax.random.fold_in(key, 11)
    first_key, second_key = jax.random.split(key)
    counts = jax.random.randint(first_key, (DEVS, PEERS), 1, CAP + 1)
    own_part = jnp.arange(DEVS) % PEERS
    full_peer = (own_part + 1 + jax.random.randint(second_key, (DEVS,), 0, PEERS - 1)) % PEERS
    columns = jnp.arange(PEERS)[None, :]
    counts = jnp.where(columns == full_peer[:, None], CAP, counts)
    counts = jnp.where(columns == own_part[:, None], 0, counts)
    return counts.astype(jnp.int32)


def draw_cross_count(key, part):
    key = jax.random.fold_in(key, 13)
    first_key, second_key = jax.random.split(key)
    counts = jax.random.randint(first_key, (DEVS,), 1, XS + 1)
    chosen = jax.random.randint(second_key, (), 0, DEVS)
    counts = jnp.where(jnp.arange(DEVS) == chosen, XS, counts)
    return counts.astype(jnp.int32)


def plant(drawn, rng, least, top_value):
    shape = drawn.shape
    place = [jax.random.randint(jax.random.fold_in(rng, axis), (), 0, shape[axis]) for axis in range(len(shape))]
    drawn = drawn.at[tuple(place)].set(least)
    longest = shape.index(max(shape))
    place[longest] = (place[longest] + 1) % shape[longest]
    return drawn.at[tuple(place)].set(top_value)


def block_levels(stream_key, extent, pieces, low, largest):
    factor_of, own = 1.0, jax.random.fold_in(stream_key, 6)
    for dim, shards_of in pieces:
        draws = jnp.exp(jax.random.uniform(jax.random.fold_in(own, dim), (shards_of,), jnp.float32, low / len(pieces), largest / len(pieces)))
        factor_of = factor_of * jnp.repeat(draws, extent[dim] // shards_of).reshape([-1 if axis == dim else 1 for axis in range(len(extent))])
    return factor_of


def normal_values(own_key, extent, width, bound, cuts=(), held_as=jnp.bfloat16):
    values = width * jax.random.normal(own_key, extent, jnp.float32)
    if cuts:
        values = values * block_levels(own_key, extent, cuts, -0.22, 0.18)
    return jnp.clip(values, -bound, bound).astype(held_as)


def setup_inputs(seed: int = 0, part: int = 0) -> dict:
    seeds = jax.random.split(jax.random.key(seed), 18)
    own_keys = jax.random.split(jax.random.fold_in(seeds[17], part), 18)
    return {
        "features": normal_values(own_keys[0], (NODES, D), 1.0, 6.0, ((0, 16),)),
        "aggregated": normal_values(own_keys[1], (NODES, D), 1.0, 6.0, ((0, 16),)),
        "cotangent": normal_values(own_keys[2], (NODES, D), 1.0, 6.0, ((0, 16),)),
        "w_self": normal_values(seeds[3], (D, D), D ** -0.5, 0.375),
        "w_neigh": normal_values(seeds[4], (D, D), D ** -0.5, 0.375),
        "tile_values": normal_values(own_keys[5], (DEVS, LT, 128, 128), (128 * TPB) ** -0.5, 0.25, ((0, 16),)),
        "tile_source": draw_tile_source(jax.random.fold_in(jax.random.fold_in(seeds[17], part), 71), part),
        "slot_source": plant(jax.random.randint(own_keys[7], (DEVS, PEERS, CAP, K), 0, ROWS), jax.random.fold_in(own_keys[7], 1), 0, ROWS - 1).astype(jnp.int32),
        "slot_weight": jnp.clip(0.25 + 0.75 * jax.random.uniform(own_keys[8], (DEVS, PEERS, CAP, K), jnp.float32) ** block_levels(own_keys[8], (DEVS, PEERS, CAP, K), ((0, 16),), -0.2, 0.2), 0.25, 1.0),
        "send_count": draw_send_count(jax.random.fold_in(jax.random.fold_in(seeds[17], part), 71), part),
        "recv_rows": plant(jax.random.randint(own_keys[10], (DEVS, PEERS, CAP), 0, ROWS), jax.random.fold_in(own_keys[10], 1), 0, ROWS - 1).astype(jnp.int32),
        "stale_grad": normal_values(own_keys[11], (DEVS, 2, XR, D), 1.0, 6.0, ((0, 16),)),
        "version": plant(jax.random.randint(own_keys[12], (DEVS,), 0, 2), jax.random.fold_in(own_keys[12], 1), 0, 1).astype(jnp.int32),
        "cross_source": plant(jax.random.randint(own_keys[13], (DEVS, XS, K), 0, XR), jax.random.fold_in(own_keys[13], 1), 0, XR - 1).astype(jnp.int32),
        "cross_weight": jnp.clip(0.25 + 0.75 * jax.random.uniform(own_keys[14], (DEVS, XS, K), jnp.float32) ** block_levels(own_keys[14], (DEVS, XS, K), ((0, 16),), -0.2, 0.2), 0.25, 1.0),
        "cross_count": draw_cross_count(jax.random.fold_in(jax.random.fold_in(seeds[17], part), 71), part),
        "cross_rows": plant(jax.random.randint(own_keys[16], (DEVS, XS), 0, ROWS), jax.random.fold_in(own_keys[16], 1), 0, ROWS - 1).astype(jnp.int32),
    }


def silu_slope(preact):
    sigmoid = jax.nn.sigmoid(preact)
    return sigmoid * (1.0 + preact * (1.0 - sigmoid))

def reference(features, aggregated, cotangent, w_self, w_neigh, tile_values, tile_source, slot_source, slot_weight, send_count, recv_rows, stale_grad, version, cross_source, cross_weight, cross_count, cross_rows):
    blocks = ROWS // 128
    self_weight = w_self.astype(jnp.float32)
    neigh_weight = w_neigh.astype(jnp.float32)
    feat_dev = features.reshape(DEVS, ROWS, D)
    aggr_dev = aggregated.reshape(DEVS, ROWS, D)
    cot_dev = cotangent.reshape(DEVS, ROWS, D)

    def forward_part(inputs):
        feat_rows, aggr_rows, cot_rows = inputs
        preact = jnp.dot(feat_rows.astype(jnp.float32), self_weight, preferred_element_type=jnp.float32) + jnp.dot(aggr_rows.astype(jnp.float32), neigh_weight, preferred_element_type=jnp.float32)
        return (cot_rows.astype(jnp.float32) * silu_slope(preact)).astype(jnp.bfloat16)
    pre_grad = lax.map(forward_part, (feat_dev, aggr_dev, cot_dev))

    def local_part(inputs):
        grad_rows, tile_vals, tile_src, slot_src, slot_wt, counts = inputs
        grad_wide = grad_rows.astype(jnp.float32)
        self_term = jnp.dot(grad_wide, self_weight.T, preferred_element_type=jnp.float32)
        neigh_grad = jnp.dot(grad_wide, neigh_weight.T, preferred_element_type=jnp.float32).astype(jnp.bfloat16)
        dest_rows = neigh_grad.reshape(blocks, 128, D).astype(jnp.float32)
        tile_block = tile_vals.reshape(blocks, TPB, 128, 128).astype(jnp.float32)
        products = jnp.einsum('btij,bid->btjd', tile_block, dest_rows).reshape(LT, 128, D)
        local_term = jax.ops.segment_sum(products, tile_src.astype(jnp.int32), num_segments=blocks).reshape(ROWS, D)
        picked = neigh_grad[slot_src].astype(jnp.float32)
        live_mask = (jnp.arange(CAP)[None, :] < counts[:, None]).astype(jnp.float32)
        outgoing = (lax.optimization_barrier(jnp.sum(picked * slot_wt[:, :, :, None], axis=2)) * live_mask[:, :, None]).astype(jnp.bfloat16)
        return (self_term + local_term, outgoing)
    base_rows, outgoing = lax.map(local_part, (pre_grad, tile_values, tile_source, slot_source, slot_weight, send_count))

    def stale_part(inputs):
        stored, which, cross_src, cross_wt, live_count = inputs
        chosen = lax.dynamic_index_in_dim(stored, which.astype(jnp.int32), 0, keepdims=False)
        stale_neigh = jnp.dot(chosen.astype(jnp.float32), neigh_weight.T, preferred_element_type=jnp.float32).astype(jnp.bfloat16)
        picked = stale_neigh[cross_src].astype(jnp.float32)
        live_mask = (jnp.arange(XS) < live_count).astype(jnp.float32)
        return (lax.optimization_barrier(jnp.sum(picked * cross_wt[:, :, None], axis=1)) * live_mask[:, None]).astype(jnp.bfloat16)
    cross_out = lax.map(stale_part, (stale_grad, version, cross_source, cross_weight, cross_count))
    incoming = outgoing.reshape(N_HST, PEERS, PEERS, CAP, D).transpose(0, 2, 1, 3, 4).reshape(DEVS, PEERS, CAP, D)
    stale_in = cross_out.reshape(N_HST, PEERS, XS, D)[::-1].reshape(DEVS, XS, D)

    def finish_part(inputs):
        base, fresh, fresh_rows, stale, stale_rows = inputs
        accum_rows = base.at[fresh_rows.reshape(-1)].add(fresh.reshape(-1, D).astype(jnp.float32))
        accum_rows = accum_rows.at[stale_rows].add(stale.astype(jnp.float32))
        return accum_rows.astype(jnp.bfloat16)
    input_grad = lax.map(finish_part, (base_rows, incoming, recv_rows, stale_in, cross_rows)).reshape(NODES, D)

    def grad_step(carry, inputs):
        feat_rows, aggr_rows, grad_rows = inputs
        grad_wide = grad_rows.astype(jnp.float32)
        self_part = jnp.dot(feat_rows.astype(jnp.float32).T, grad_wide, preferred_element_type=jnp.float32)
        neigh_part = jnp.dot(aggr_rows.astype(jnp.float32).T, grad_wide, preferred_element_type=jnp.float32)
        return (carry + jnp.stack([self_part, neigh_part]), None)
    summed, unused = lax.scan(grad_step, jnp.zeros((2, D, D), jnp.float32), (feat_dev, aggr_dev, pre_grad))
    weight_grads = (summed * (1.0 / math.sqrt(NODES))).astype(jnp.bfloat16)
    return (input_grad, weight_grads)
```

```python
import functools
import math

import jax
import jax.numpy as jnp
from jax import lax
from jax.experimental import pallas as pl
from jax.experimental.pallas import tpu as pltpu
from jax.sharding import PartitionSpec as P

BF16, F32 = jnp.bfloat16, jnp.float32
VMEM = pl.BlockSpec(memory_space=pltpu.VMEM)
SMEM = pl.BlockSpec(memory_space=pltpu.SMEM)
PARAMS = pltpu.CompilerParams(vmem_limit_bytes=40 * 2**20)
NT = (((1,), (1,)), ((), ()))
TN = (((0,), (0,)), ((), ()))


def swap(value, axis, bit):
    pairs = [(source, source ^ (1 << bit)) for source in range(lax.axis_size(axis))]
    return lax.ppermute(value, axis, pairs)


def silu_slope(preact):
    sigmoid = jax.nn.sigmoid(preact)
    return sigmoid * (1.0 + preact * (1.0 - sigmoid))


def bit_reversed(count):
    bits = count.bit_length() - 1
    return [sum(((r >> b) & 1) << (bits - 1 - b) for b in range(bits)) for r in range(count)]


def split_dot(weights, rows):
    high = weights.astype(BF16)
    low = (weights - high.astype(F32)).astype(BF16)
    return jnp.dot(high, rows, preferred_element_type=F32) + jnp.dot(
        low, rows, preferred_element_type=F32
    )


def outgoing_kernel(
    me_ref, count_ref, grad_ref, weight_ref, source_ref, scale_ref, neigh_ref, out_ref
):
    peers, fan, cap = source_ref.shape
    me = me_ref[0]
    neigh = lax.dot_general(grad_ref[...], weight_ref[...], NT, preferred_element_type=F32)
    neigh = neigh.astype(BF16)
    neigh_ref[...] = neigh
    rows = neigh.shape[0]
    order = bit_reversed(peers)
    slot = lax.broadcasted_iota(jnp.int32, (fan, cap), 1)
    group = min(peers, 128 // cap)
    for first in range(0, peers, group):
        sources, scales = [], []
        for r in order[first : first + group]:
            q = jnp.bitwise_xor(me, r)
            live = slot < count_ref[0, q]
            sources.append(source_ref[q])
            scales.append(jnp.where(live, scale_ref[q], 0.0))
        sources = jnp.concatenate(sources, axis=1).T
        scales = jnp.concatenate(scales, axis=1).T
        slots = group * cap
        node = lax.broadcasted_iota(jnp.int32, (slots, rows), 1)
        select = jnp.zeros((slots, rows), F32)
        for k in range(fan):
            select += jnp.where(sources[:, k : k + 1] == node, scales[:, k : k + 1], 0.0)
        out_ref[pl.ds(first * cap, slots), :] = split_dot(select, neigh).astype(BF16)


def stale_kernel(version_ref, count_ref, stale_ref, weight_ref, source_ref, scale_ref, out_ref):
    chosen = stale_ref[version_ref[0]]
    neigh = lax.dot_general(chosen, weight_ref[...], NT, preferred_element_type=F32).astype(BF16)
    fan, slots = source_ref.shape
    slot = lax.broadcasted_iota(jnp.int32, (1, slots), 1)
    live = slot < count_ref[0]
    stored = lax.broadcasted_iota(jnp.int32, (neigh.shape[0], slots), 0)
    select = jnp.zeros(stored.shape, F32)
    for k in range(fan):
        scale = jnp.where(live, scale_ref[pl.ds(k, 1), :], 0.0)
        select += jnp.where(source_ref[pl.ds(k, 1), :] == stored, scale, 0.0)
    out_ref[...] = split_dot(select.T, neigh).astype(BF16)


def local_kernel(source_ref, grad_ref, neigh_ref, weight_ref, tile_ref, base_ref):
    blocks = base_ref.shape[0]
    tiles = tile_ref.shape[0]
    per_block = tiles // blocks
    for b in range(blocks):
        rows = pl.ds(b * 128, 128)
        base_ref[b] = lax.dot_general(
            grad_ref[rows, :], weight_ref[...], NT, preferred_element_type=F32
        )
    for b in range(blocks):
        neigh = neigh_ref[pl.ds(b * 128, 128), :]
        for t in range(b * per_block, (b + 1) * per_block):
            product = lax.dot_general(tile_ref[t], neigh, TN, preferred_element_type=F32)
            base_ref[source_ref[0, t]] += product


def finish_kernel(me_ref, base_ref, fresh_ref, stale_ref, recv_ref, cross_ref, out_ref):
    me = me_ref[0]
    blocks = base_ref.shape[0]
    peers, cap = recv_ref.shape
    targets = [recv_ref[pl.ds(jnp.bitwise_xor(me, o), 1), :] for o in bit_reversed(peers)]
    fresh_rows = jnp.concatenate(targets, axis=1)
    stale_rows = cross_ref[...]
    for b in range(blocks):
        total = base_ref[b]
        for rows, values in ((fresh_rows, fresh_ref), (stale_rows, stale_ref)):
            node = b * 128 + lax.broadcasted_iota(jnp.int32, (128, rows.shape[1]), 0)
            hit = jnp.where(node == rows, 1.0, 0.0).astype(BF16)
            total += jnp.dot(hit, values[...], preferred_element_type=F32)
        out_ref[pl.ds(b * 128, 128), :] = total.astype(BF16)


def body(
    features,
    aggregated,
    cotangent,
    w_self,
    w_neigh,
    tile_values,
    tile_source,
    slot_source,
    slot_weight,
    send_count,
    recv_rows,
    stale_grad,
    version,
    cross_source,
    cross_weight,
    cross_count,
    cross_rows,
):
    row_count, dim = features.shape
    blocks = row_count // 128
    peers = lax.axis_size("dom")
    cap = slot_source.shape[2]
    bits = peers.bit_length() - 1
    host = lax.axis_index("hst")
    me = lax.axis_index("dom")
    me_ref = me.astype(jnp.int32).reshape(1)
    odd = (me & 1) == 1
    struct = jax.ShapeDtypeStruct

    preact = jnp.dot(features, w_self, preferred_element_type=F32) + jnp.dot(
        aggregated, w_neigh, preferred_element_type=F32
    )
    pre_grad = (cotangent.astype(F32) * silu_slope(preact)).astype(BF16)
    self_sum = jnp.einsum("rd,re->de", features, pre_grad, preferred_element_type=F32)
    neigh_sum = jnp.einsum("rd,re->de", aggregated, pre_grad, preferred_element_type=F32)

    first = host == 0
    half = jnp.where(first, self_sum, neigh_sum) + swap(
        jnp.where(first, neigh_sum, self_sum).astype(BF16), "hst", 0
    ).astype(F32)

    neigh_grad, outgoing = pl.pallas_call(
        outgoing_kernel,
        out_shape=(struct((row_count, dim), BF16), struct((peers * cap, dim), BF16)),
        in_specs=[SMEM, SMEM, VMEM, VMEM, VMEM, VMEM],
        out_specs=(VMEM, VMEM),
        compiler_params=PARAMS,
        name="outgoing",
    )(
        me_ref,
        send_count,
        pre_grad,
        w_neigh,
        jnp.swapaxes(slot_source[0], 1, 2),
        jnp.swapaxes(slot_weight[0], 1, 2),
    )
    cross_out = pl.pallas_call(
        stale_kernel,
        out_shape=struct((cross_source.shape[1], dim), BF16),
        in_specs=[SMEM, SMEM, VMEM, VMEM, VMEM, VMEM],
        out_specs=VMEM,
        compiler_params=PARAMS,
        name="stale_rows",
    )(
        version,
        cross_count,
        stale_grad[0],
        w_neigh,
        cross_source[0].T,
        cross_weight[0].T,
    )
    stale_in = swap(cross_out, "hst", 0)
    base = pl.pallas_call(
        local_kernel,
        out_shape=struct((blocks, 128, dim), F32),
        in_specs=[SMEM, VMEM, VMEM, VMEM, VMEM],
        out_specs=VMEM,
        compiler_params=PARAMS,
        name="local_term",
    )(tile_source, pre_grad, neigh_grad, w_self, tile_values[0])

    quarter = dim // 2
    held = outgoing.reshape(1, peers * cap, dim)
    for bit in range(bits):
        if bit == 0:
            low, high = half[:quarter], half[quarter:]
            kept, given = jnp.where(odd, high, low), jnp.where(odd, low, high).astype(BF16)
        else:
            given = kept.astype(BF16)
            kept = given.astype(F32)
        middle = held.shape[1] // 2
        moved = held[:, middle:].reshape(-1, dim)
        arrived = swap(jnp.concatenate([given, moved], axis=0), "dom", bit)
        kept = kept + arrived[:quarter].astype(F32)
        held = jnp.stack(
            [held[:, :middle], arrived[quarter:].reshape(-1, middle, dim)], axis=1
        ).reshape(-1, middle, dim)

    out_rows = pl.pallas_call(
        finish_kernel,
        out_shape=struct((row_count, dim), BF16),
        in_specs=[SMEM, VMEM, VMEM, VMEM, VMEM, VMEM],
        out_specs=VMEM,
        compiler_params=PARAMS,
        name="finish",
    )(me_ref, base, held.reshape(peers * cap, dim), stale_in, recv_rows[0], cross_rows)

    node_total = row_count * lax.axis_size("hst") * peers
    mine = (kept * (1.0 / math.sqrt(node_total))).astype(BF16)
    other = swap(mine, "dom", 0)
    mine = jnp.where(
        odd, jnp.concatenate([other, mine], axis=0), jnp.concatenate([mine, other], axis=0)
    )
    other = swap(mine, "hst", 0)
    sums = jnp.where(first, jnp.stack([mine, other]), jnp.stack([other, mine]))
    return (out_rows, sums)


def solution(mesh):
    rows = ("runs", "hst", "dom")
    specs = [P(rows)] * 17
    specs[3] = specs[4] = P()
    return jax.shard_map(
        body,
        mesh=mesh,
        in_specs=tuple(specs),
        out_specs=(P(rows), P("runs")),
        check_vma=False,
    )
```

```python
import functools
import math

import jax
import jax.numpy as jnp
from jax import lax
from jax.experimental import pallas as pl
from jax.experimental.pallas import tpu as pltpu
from jax.sharding import PartitionSpec as P

BF16, F32 = jnp.bfloat16, jnp.float32
VMEM = pl.BlockSpec(memory_space=pltpu.VMEM)
ANY = pl.BlockSpec(memory_space=pl.ANY)
SMEM = pl.BlockSpec(memory_space=pltpu.SMEM)
PARAMS = pltpu.CompilerParams(vmem_limit_bytes=16 * 2**20)
NT = (((1,), (1,)), ((), ()))
TN = (((0,), (0,)), ((), ()))
PARTS = 2
CHUNKS = 3
OUT_BLOCKS = 4


def in_hbm(*values):
    return [pltpu.with_memory_space_constraint(value, pltpu.HBM) for value in values]


def swap(value, axis, bit):
    pairs = [(source, source ^ (1 << bit)) for source in range(lax.axis_size(axis))]
    return lax.ppermute(value, axis, pairs)


def silu_slope(preact):
    sigmoid = jax.nn.sigmoid(preact)
    return sigmoid * (1.0 + preact * (1.0 - sigmoid))


def hop_bits(count):
    bits = count.bit_length() - 1
    return [*range(1, bits), 0]


def hop_order(count):
    hops = hop_bits(count)[::-1]
    return [sum(((i >> j) & 1) << bit for j, bit in enumerate(hops)) for i in range(count)]


def split_dot(weights, rows):
    high = weights.astype(BF16)
    low = (weights - high.astype(F32)).astype(BF16)
    return jnp.dot(high, rows, preferred_element_type=F32) + jnp.dot(
        low, rows, preferred_element_type=F32
    )


def gradient_kernel(
    host_ref,
    features_hbm,
    aggregated_hbm,
    cotangent_hbm,
    self_hbm,
    neigh_hbm,
    grad_ref,
    kept_ref,
    given_ref,
    features,
    aggregated,
    cotangent,
    self_weight,
    neigh_weight,
    sums,
    sems,
):
    part_rows = features.shape[0] // PARTS
    rows = part_rows // CHUNKS
    copies = []

    def fetch(source, target):
        copy = pltpu.make_async_copy(source, target, sems.at[len(copies)])
        copy.start()
        copies.append(copy)

    fetch(self_hbm, self_weight)
    fetch(neigh_hbm, neigh_weight)
    for p in range(PARTS):
        part = pl.ds(p * part_rows, part_rows)
        fetch(features_hbm.at[part], features.at[part])
        fetch(aggregated_hbm.at[part], aggregated.at[part])
        fetch(cotangent_hbm.at[part], cotangent.at[part])
    copies[0].wait()
    copies[1].wait()
    for p in range(PARTS):
        for copy in copies[3 * p + 2 : 3 * p + 5]:
            copy.wait()
        for c in range(CHUNKS):
            part = pl.ds(p * part_rows + c * rows, rows)
            left, right = features[part, :], aggregated[part, :]
            preact = jnp.dot(left, self_weight[...], preferred_element_type=F32) + jnp.dot(
                right, neigh_weight[...], preferred_element_type=F32
            )
            grad = (cotangent[part, :].astype(F32) * silu_slope(preact)).astype(BF16)
            grad_ref[part, :] = grad
            for i, values in enumerate((left, right)):
                term = lax.dot_general(values, grad, TN, preferred_element_type=F32)
                if p == 0 and c == 0:
                    sums[i] = term
                else:
                    sums[i] += term
    host = host_ref[0]
    kept_ref[...] = sums[host]
    given_ref[...] = sums[1 - host].astype(BF16)


def outgoing_kernel(
    me_ref,
    count_ref,
    grad_ref,
    weight_ref,
    source_ref,
    scale_ref,
    after_ref,
    neigh_ref,
    out_ref,
):
    peers, fan, cap = source_ref.shape
    me = me_ref[0]
    neigh = lax.dot_general(grad_ref[...], weight_ref[...], NT, preferred_element_type=F32)
    neigh = neigh.astype(BF16)
    neigh_ref[...] = neigh
    rows = neigh.shape[0]
    order = hop_order(peers)
    slot = lax.broadcasted_iota(jnp.int32, (fan, cap), 1)
    group = min(peers, 128 // cap)
    for first in range(0, peers, group):
        sources, scales = [], []
        for r in order[first : first + group]:
            q = jnp.bitwise_xor(me, r)
            live = slot < count_ref[0, q]
            sources.append(source_ref[q])
            scales.append(jnp.where(live, scale_ref[q], 0.0))
        sources = jnp.concatenate(sources, axis=1).T
        scales = jnp.concatenate(scales, axis=1).T
        slots = group * cap
        node = lax.broadcasted_iota(jnp.int32, (slots, rows), 1)
        select = jnp.zeros((slots, rows), F32)
        for k in range(fan):
            select += jnp.where(sources[:, k : k + 1] == node, scales[:, k : k + 1], 0.0)
        out_ref[pl.ds(first * cap, slots), :] = split_dot(select, neigh).astype(BF16)


def stale_kernel(
    version_ref, count_ref, stale_ref, weight_ref, source_ref, scale_ref, stay_ref, out_ref, same_ref
):
    chosen = stale_ref[version_ref[0]]
    neigh = lax.dot_general(chosen, weight_ref[...], NT, preferred_element_type=F32).astype(BF16)
    fan, slots = source_ref.shape
    live = lax.broadcasted_iota(jnp.int32, (1, slots), 1) < count_ref[0]
    stored = lax.broadcasted_iota(jnp.int32, (neigh.shape[0], slots), 0)
    select = jnp.zeros(stored.shape, F32)
    for k in range(fan):
        scale = jnp.where(live, scale_ref[pl.ds(k, 1), :], 0.0)
        select += jnp.where(source_ref[pl.ds(k, 1), :] == stored, scale, 0.0)
    out_ref[...] = split_dot(select.T, neigh).astype(BF16)


def local_kernel(
    source_ref,
    grad_ref,
    neigh_ref,
    weight_ref,
    tile_ref,
    stay_ref,
    base_ref,
    same_ref,
):
    blocks = base_ref.shape[0]
    tiles = tile_ref.shape[0]
    per_block = tiles // blocks
    for b in range(blocks):
        rows = pl.ds(b * 128, 128)
        base_ref[b] = lax.dot_general(
            grad_ref[rows, :], weight_ref[...], NT, preferred_element_type=F32
        )
    for b in range(blocks):
        neigh = neigh_ref[pl.ds(b * 128, 128), :]
        for t in range(b * per_block, (b + 1) * per_block):
            product = lax.dot_general(tile_ref[t], neigh, TN, preferred_element_type=F32)
            base_ref[source_ref[0, t]] += product


def finish_kernel(
    me_ref, base_ref, fresh_ref, stale_ref, recv_ref, cross_ref, out_hbm, out, sems
):
    me = me_ref[0]
    blocks = base_ref.shape[0]
    peers, cap = recv_ref.shape
    targets = [recv_ref[pl.ds(jnp.bitwise_xor(me, o), 1), :] for o in hop_order(peers)]
    targets = jnp.concatenate(targets + [cross_ref[...]], axis=1)
    values = jnp.concatenate([fresh_ref[...], stale_ref[...]], axis=0)
    copies = []
    for b in range(blocks):
        node = b * 128 + lax.broadcasted_iota(jnp.int32, (128, targets.shape[1]), 0)
        hit = jnp.where(node == targets, 1.0, 0.0).astype(BF16)
        total = base_ref[b] + jnp.dot(hit, values, preferred_element_type=F32)
        out[pl.ds(b * 128, 128), :] = total.astype(BF16)
        if (b + 1) % OUT_BLOCKS == 0 or b + 1 == blocks:
            first = b // OUT_BLOCKS * OUT_BLOCKS
            part = pl.ds(first * 128, (b + 1 - first) * 128)
            copy = pltpu.make_async_copy(out.at[part], out_hbm.at[part], sems.at[len(copies)])
            copy.start()
            copies.append(copy)
    for copy in copies:
        copy.wait()


def body(
    features,
    aggregated,
    cotangent,
    w_self,
    w_neigh,
    tile_values,
    tile_source,
    slot_source,
    slot_weight,
    send_count,
    recv_rows,
    stale_grad,
    version,
    cross_source,
    cross_weight,
    cross_count,
    cross_rows,
):
    row_count, dim = features.shape
    blocks = row_count // 128
    peers = lax.axis_size("dom")
    cap = slot_source.shape[2]
    bits = peers.bit_length() - 1
    host = lax.axis_index("hst")
    me = lax.axis_index("dom")
    me_ref = me.astype(jnp.int32).reshape(1)
    host_ref = host.astype(jnp.int32).reshape(1)
    odd = (me & 1) == 1
    struct = jax.ShapeDtypeStruct

    pre_grad, own, given = pl.pallas_call(
        gradient_kernel,
        out_shape=(
            pltpu.VMEM((row_count, dim), BF16),
            pltpu.VMEM((dim, dim), F32),
            pltpu.VMEM((dim, dim), BF16),
        ),
        in_specs=[SMEM, ANY, ANY, ANY, ANY, ANY],
        out_specs=(VMEM, VMEM, VMEM),
        scratch_shapes=[
            pltpu.VMEM((row_count, dim), BF16),
            pltpu.VMEM((row_count, dim), BF16),
            pltpu.VMEM((row_count, dim), BF16),
            pltpu.VMEM((dim, dim), BF16),
            pltpu.VMEM((dim, dim), BF16),
            pltpu.VMEM((2, dim, dim), F32),
            pltpu.SemaphoreType.DMA((2 + 3 * PARTS,)),
        ],
        compiler_params=PARAMS,
        name="gradients",
    )(host_ref, *in_hbm(features, aggregated, cotangent, w_self, w_neigh))
    first = host == 0
    half = own + swap(given, "hst", 0).astype(F32)
    quarter = dim // 2
    low, high = half[:quarter], half[quarter:]
    kept, given = jnp.where(odd, high, low), jnp.where(odd, low, high).astype(BF16)
    kept = kept + swap(given, "dom", 0).astype(F32)

    neigh_grad, outgoing = pl.pallas_call(
        outgoing_kernel,
        out_shape=(struct((row_count, dim), BF16), struct((peers * cap, dim), BF16)),
        in_specs=[SMEM, SMEM, VMEM, VMEM, VMEM, VMEM, ANY],
        out_specs=(VMEM, VMEM),
        compiler_params=PARAMS,
        name="outgoing",
    )(
        me_ref,
        send_count,
        pre_grad,
        w_neigh,
        jnp.swapaxes(slot_source[0], 1, 2),
        jnp.swapaxes(slot_weight[0], 1, 2),
        given,
    )
    held = outgoing.reshape(1, peers * cap, dim)
    scale = 1.0 / math.sqrt(row_count * lax.axis_size("hst") * peers)
    for step, bit in enumerate(hop_bits(peers)):
        given = (kept if bit else kept * scale).astype(BF16)
        middle = held.shape[1] // 2
        stay, moved = held[:, :middle], held[:, middle:].reshape(-1, dim)
        arrived = swap(jnp.concatenate([given, moved], axis=0), "dom", bit)
        if step == 0:
            cross_out, stay = pl.pallas_call(
                stale_kernel,
                out_shape=(
                    struct((cross_source.shape[1], dim), BF16),
                    struct(stay.shape, stay.dtype),
                ),
                in_specs=[SMEM, SMEM, VMEM, VMEM, VMEM, VMEM, ANY],
                out_specs=(VMEM, ANY),
                input_output_aliases={6: 1},
                compiler_params=PARAMS,
                name="stale_rows",
            )(
                version,
                cross_count,
                stale_grad[0],
                w_neigh,
                cross_source[0].T,
                cross_weight[0].T,
                stay,
            )
            stale_in = swap(cross_out, "hst", 0)
        if step == 1:
            base, stay = pl.pallas_call(
                local_kernel,
                out_shape=(
                    struct((blocks, 128, dim), F32),
                    struct(stay.shape, stay.dtype),
                ),
                in_specs=[SMEM, VMEM, VMEM, VMEM, VMEM, ANY],
                out_specs=(VMEM, ANY),
                input_output_aliases={5: 1},
                compiler_params=PARAMS,
                name="local_term",
            )(tile_source, pre_grad, neigh_grad, w_self, tile_values[0], stay)
        other = arrived[:quarter]
        kept = given.astype(F32) + other.astype(F32)
        held = jnp.stack([stay, arrived[quarter:].reshape(stay.shape)], axis=1)
        held = held.reshape(-1, middle, dim)
    mine = jnp.where(
        odd, jnp.concatenate([other, given], axis=0), jnp.concatenate([given, other], axis=0)
    )
    other = swap(mine, "hst", 0)
    sums = jnp.where(first, jnp.stack([mine, other]), jnp.stack([other, mine]))

    out_rows = pl.pallas_call(
        finish_kernel,
        out_shape=struct((row_count, dim), BF16),
        in_specs=[SMEM, VMEM, VMEM, VMEM, VMEM, VMEM],
        out_specs=ANY,
        scratch_shapes=[
            pltpu.VMEM((row_count, dim), BF16),
            pltpu.SemaphoreType.DMA((pl.cdiv(blocks, OUT_BLOCKS),)),
        ],
        compiler_params=PARAMS,
        name="finish",
    )(me_ref, base, held.reshape(peers * cap, dim), stale_in, recv_rows[0], cross_rows)
    return (out_rows, sums)


def solution(mesh):
    rows = ("runs", "hst", "dom")
    specs = [P(rows)] * 17
    specs[3] = specs[4] = P()
    return jax.shard_map(
        body,
        mesh=mesh,
        in_specs=tuple(specs),
        out_specs=(P(rows), P("runs")),
        check_vma=False,
    )
```

```python
import functools
import math

import jax
import jax.numpy as jnp
from jax import lax
from jax.experimental import pallas as pl
from jax.experimental.pallas import tpu as pltpu
from jax.sharding import PartitionSpec as P

BF16, F32 = jnp.bfloat16, jnp.float32
VMEM = pl.BlockSpec(memory_space=pltpu.VMEM)
ANY = pl.BlockSpec(memory_space=pl.ANY)
SMEM = pl.BlockSpec(memory_space=pltpu.SMEM)
PARAMS = pltpu.CompilerParams(vmem_limit_bytes=16 * 2**20)
NT = (((1,), (1,)), ((), ()))
TN = (((0,), (0,)), ((), ()))
PARTS = 2
CHUNKS = 3
OUT_BLOCKS = 2


def in_hbm(*values):
    return [pltpu.with_memory_space_constraint(value, pltpu.HBM) for value in values]


def swap(value, axis, bit):
    pairs = [(source, source ^ (1 << bit)) for source in range(lax.axis_size(axis))]
    return lax.ppermute(value, axis, pairs)


def silu_slope(preact):
    sigmoid = jax.nn.sigmoid(preact)
    return sigmoid * (1.0 + preact * (1.0 - sigmoid))


def hop_bits(count):
    bits = count.bit_length() - 1
    return [*range(1, bits), 0]


def hop_order(count):
    hops = hop_bits(count)[::-1]
    return [sum(((i >> j) & 1) << bit for j, bit in enumerate(hops)) for i in range(count)]


def split_dot(weights, rows):
    high = weights.astype(BF16)
    low = (weights - high.astype(F32)).astype(BF16)
    return jnp.dot(high, rows, preferred_element_type=F32) + jnp.dot(
        low, rows, preferred_element_type=F32
    )


def gradient_kernel(
    features_hbm,
    aggregated_hbm,
    cotangent_hbm,
    self_hbm,
    neigh_hbm,
    inputs_ref,
    grad_ref,
    given_ref,
    cotangent,
    self_weight,
    neigh_weight,
    turned,
    sems,
):
    part_rows = cotangent.shape[0] // PARTS
    rows = part_rows // CHUNKS
    copies = []

    def fetch(source, target):
        copy = pltpu.make_async_copy(source, target, sems.at[len(copies)])
        copy.start()
        copies.append(copy)

    fetch(self_hbm, self_weight)
    fetch(neigh_hbm, neigh_weight)
    for p in range(PARTS):
        part = pl.ds(p * part_rows, part_rows)
        fetch(features_hbm.at[part], inputs_ref.at[0, part])
        fetch(aggregated_hbm.at[part], inputs_ref.at[1, part])
        fetch(cotangent_hbm.at[part], cotangent.at[part])
    copies[0].wait()
    copies[1].wait()
    other = 1 - lax.axis_index("hst")
    for p in range(PARTS):
        for copy in copies[3 * p + 2 : 3 * p + 5]:
            copy.wait()
        for c in range(CHUNKS):
            part = pl.ds(p * part_rows + c * rows, rows)
            left, right = inputs_ref[0, part, :], inputs_ref[1, part, :]
            preact = jnp.dot(left, self_weight[...], preferred_element_type=F32) + jnp.dot(
                right, neigh_weight[...], preferred_element_type=F32
            )
            grad = (cotangent[part, :].astype(F32) * silu_slope(preact)).astype(BF16)
            grad_ref[part, :] = grad
            turned[:, part] = jnp.where(other == 0, left, right).T
    given_ref[...] = jnp.dot(
        turned[...], grad_ref[...], preferred_element_type=F32
    ).astype(BF16)


def kept_kernel(inputs_ref, grad_ref, after_ref, kept_ref):
    host = lax.axis_index("hst")
    kept_ref[...] = lax.dot_general(
        inputs_ref[host], grad_ref[...], TN, preferred_element_type=F32
    )


def outgoing_kernel(
    count_ref,
    grad_ref,
    weight_ref,
    source_ref,
    scale_ref,
    after_ref,
    neigh_ref,
    out_ref,
):
    peers, fan, cap = source_ref.shape
    me = lax.axis_index("dom")
    neigh = lax.dot_general(grad_ref[...], weight_ref[...], NT, preferred_element_type=F32)
    neigh = neigh.astype(BF16)
    neigh_ref[...] = neigh
    rows = neigh.shape[0]
    order = hop_order(peers)
    slot = lax.broadcasted_iota(jnp.int32, (fan, cap), 1)
    group = min(peers, 128 // cap)
    for first in range(0, peers, group):
        sources, scales = [], []
        for r in order[first : first + group]:
            q = jnp.bitwise_xor(me, r)
            live = slot < count_ref[0, q]
            sources.append(source_ref[q])
            scales.append(jnp.where(live, scale_ref[q], 0.0))
        sources = jnp.concatenate(sources, axis=1).T
        scales = jnp.concatenate(scales, axis=1).T
        slots = group * cap
        node = lax.broadcasted_iota(jnp.int32, (slots, rows), 1)
        select = jnp.zeros((slots, rows), F32)
        for k in range(fan):
            select += jnp.where(sources[:, k : k + 1] == node, scales[:, k : k + 1], 0.0)
        out_ref[pl.ds(first * cap, slots), :] = split_dot(select, neigh).astype(BF16)


def stale_kernel(
    version_ref, count_ref, stale_ref, weight_ref, source_ref, scale_ref, stay_ref, out_ref, same_ref
):
    chosen = stale_ref[version_ref[0]]
    neigh = lax.dot_general(chosen, weight_ref[...], NT, preferred_element_type=F32).astype(BF16)
    fan, slots = source_ref.shape
    live = lax.broadcasted_iota(jnp.int32, (1, slots), 1) < count_ref[0]
    stored = lax.broadcasted_iota(jnp.int32, (neigh.shape[0], slots), 0)
    select = jnp.zeros(stored.shape, F32)
    for k in range(fan):
        scale = jnp.where(live, scale_ref[pl.ds(k, 1), :], 0.0)
        select += jnp.where(source_ref[pl.ds(k, 1), :] == stored, scale, 0.0)
    out_ref[...] = split_dot(select.T, neigh).astype(BF16)


def local_kernel(
    source_ref,
    grad_ref,
    neigh_ref,
    weight_ref,
    tile_ref,
    stay_ref,
    base_ref,
    same_ref,
):
    blocks = base_ref.shape[0]
    tiles = tile_ref.shape[0]
    per_block = tiles // blocks
    for b in range(blocks):
        rows = pl.ds(b * 128, 128)
        base_ref[b] = lax.dot_general(
            grad_ref[rows, :], weight_ref[...], NT, preferred_element_type=F32
        )
    for b in range(blocks):
        neigh = neigh_ref[pl.ds(b * 128, 128), :]
        for t in range(b * per_block, (b + 1) * per_block):
            product = lax.dot_general(tile_ref[t], neigh, TN, preferred_element_type=F32)
            base_ref[source_ref[0, t]] += product


def finish_kernel(
    base_ref, fresh_ref, stale_ref, recv_ref, cross_ref, out_hbm, out, sems
):
    me = lax.axis_index("dom")
    blocks = base_ref.shape[0]
    peers, cap = recv_ref.shape
    targets = [recv_ref[pl.ds(jnp.bitwise_xor(me, o), 1), :] for o in hop_order(peers)]
    targets = jnp.concatenate(targets + [cross_ref[...]], axis=1)
    values = jnp.concatenate([fresh_ref[...], stale_ref[...]], axis=0)
    copies = []
    for b in range(blocks):
        node = b * 128 + lax.broadcasted_iota(jnp.int32, (128, targets.shape[1]), 0)
        hit = jnp.where(node == targets, 1.0, 0.0).astype(BF16)
        total = base_ref[b] + jnp.dot(hit, values, preferred_element_type=F32)
        out[pl.ds(b * 128, 128), :] = total.astype(BF16)
        if (b + 1) % OUT_BLOCKS == 0 or b + 1 == blocks:
            first = b // OUT_BLOCKS * OUT_BLOCKS
            part = pl.ds(first * 128, (b + 1 - first) * 128)
            copy = pltpu.make_async_copy(out.at[part], out_hbm.at[part], sems.at[len(copies)])
            copy.start()
            copies.append(copy)
    for copy in copies:
        copy.wait()


def sums_kernel(mine_ref, other_ref, out_hbm, sems):
    host = lax.axis_index("hst")
    copies = [
        pltpu.make_async_copy(mine_ref, out_hbm.at[host], sems.at[0]),
        pltpu.make_async_copy(other_ref, out_hbm.at[1 - host], sems.at[1]),
    ]
    for copy in copies:
        copy.start()
    for copy in copies:
        copy.wait()


def body(
    features,
    aggregated,
    cotangent,
    w_self,
    w_neigh,
    tile_values,
    tile_source,
    slot_source,
    slot_weight,
    send_count,
    recv_rows,
    stale_grad,
    version,
    cross_source,
    cross_weight,
    cross_count,
    cross_rows,
):
    row_count, dim = features.shape
    blocks = row_count // 128
    peers = lax.axis_size("dom")
    cap = slot_source.shape[2]
    bits = peers.bit_length() - 1
    host = lax.axis_index("hst")
    me = lax.axis_index("dom")
    odd = (me & 1) == 1
    struct = jax.ShapeDtypeStruct

    inputs, pre_grad, given = pl.pallas_call(
        gradient_kernel,
        out_shape=(
            pltpu.VMEM((2, row_count, dim), BF16),
            pltpu.VMEM((row_count, dim), BF16),
            pltpu.VMEM((dim, dim), BF16),
        ),
        in_specs=[ANY] * 5,
        out_specs=(VMEM, VMEM, VMEM),
        scratch_shapes=[
            pltpu.VMEM((row_count, dim), BF16),
            pltpu.VMEM((dim, dim), BF16),
            pltpu.VMEM((dim, dim), BF16),
            pltpu.VMEM((dim, row_count), BF16),
            pltpu.SemaphoreType.DMA((2 + 3 * PARTS,)),
        ],
        compiler_params=PARAMS,
        name="gradients",
    )(*in_hbm(features, aggregated, cotangent, w_self, w_neigh))
    own = pl.pallas_call(
        kept_kernel,
        out_shape=pltpu.VMEM((dim, dim), F32),
        in_specs=[VMEM, VMEM, ANY],
        out_specs=VMEM,
        compiler_params=PARAMS,
        name="kept_sum",
    )(inputs, pre_grad, given)

    first = host == 0
    half = own + swap(given, "hst", 0).astype(F32)
    quarter = dim // 2
    low, high = half[:quarter], half[quarter:]
    kept, given = jnp.where(odd, high, low), jnp.where(odd, low, high).astype(BF16)
    kept = kept + swap(given, "dom", 0).astype(F32)

    neigh_grad, outgoing = pl.pallas_call(
        outgoing_kernel,
        out_shape=(struct((row_count, dim), BF16), struct((peers * cap, dim), BF16)),
        in_specs=[SMEM, VMEM, VMEM, VMEM, VMEM, ANY],
        out_specs=(VMEM, VMEM),
        compiler_params=PARAMS,
        name="outgoing",
    )(
        send_count,
        pre_grad,
        w_neigh,
        jnp.swapaxes(slot_source[0], 1, 2),
        jnp.swapaxes(slot_weight[0], 1, 2),
        given,
    )
    held = outgoing.reshape(1, peers * cap, dim)
    scale = 1.0 / math.sqrt(row_count * lax.axis_size("hst") * peers)
    for step, bit in enumerate(hop_bits(peers)):
        given = (kept if bit else kept * scale).astype(BF16)
        middle = held.shape[1] // 2
        stay, moved = held[:, :middle], held[:, middle:].reshape(-1, dim)
        arrived = swap(jnp.concatenate([given, moved], axis=0), "dom", bit)
        if step == 0:
            cross_out, stay = pl.pallas_call(
                stale_kernel,
                out_shape=(
                    struct((cross_source.shape[1], dim), BF16),
                    struct(stay.shape, stay.dtype),
                ),
                in_specs=[SMEM, SMEM, VMEM, VMEM, VMEM, VMEM, ANY],
                out_specs=(VMEM, ANY),
                input_output_aliases={6: 1},
                compiler_params=PARAMS,
                name="stale_rows",
            )(
                version,
                cross_count,
                stale_grad[0],
                w_neigh,
                cross_source[0].T,
                cross_weight[0].T,
                stay,
            )
            stale_in = swap(cross_out, "hst", 0)
        if step == 1:
            base, stay = pl.pallas_call(
                local_kernel,
                out_shape=(
                    struct((blocks, 128, dim), F32),
                    struct(stay.shape, stay.dtype),
                ),
                in_specs=[SMEM, VMEM, VMEM, VMEM, VMEM, ANY],
                out_specs=(VMEM, ANY),
                input_output_aliases={5: 1},
                compiler_params=PARAMS,
                name="local_term",
            )(tile_source, pre_grad, neigh_grad, w_self, tile_values[0], stay)
        other = arrived[:quarter]
        kept = given.astype(F32) + other.astype(F32)
        held = jnp.stack([stay, arrived[quarter:].reshape(stay.shape)], axis=1)
        held = held.reshape(-1, middle, dim)
    mine = jnp.where(
        odd, jnp.concatenate([other, given], axis=0), jnp.concatenate([given, other], axis=0)
    )
    other = swap(mine, "hst", 0)
    sums = pl.pallas_call(
        sums_kernel,
        out_shape=struct((2, dim, dim), BF16),
        in_specs=[VMEM, VMEM],
        out_specs=ANY,
        scratch_shapes=[pltpu.SemaphoreType.DMA((2,))],
        compiler_params=PARAMS,
        name="weight_grads",
    )(mine, other)

    out_rows = pl.pallas_call(
        finish_kernel,
        out_shape=struct((row_count, dim), BF16),
        in_specs=[VMEM] * 5,
        out_specs=ANY,
        scratch_shapes=[
            pltpu.VMEM((row_count, dim), BF16),
            pltpu.SemaphoreType.DMA((pl.cdiv(blocks, OUT_BLOCKS),)),
        ],
        compiler_params=PARAMS,
        name="finish",
    )(base, held.reshape(peers * cap, dim), stale_in, recv_rows[0], cross_rows)
    return (out_rows, sums)


def solution(mesh):
    rows = ("runs", "hst", "dom")
    specs = [P(rows)] * 17
    specs[3] = specs[4] = P()
    return jax.shard_map(
        body,
        mesh=mesh,
        in_specs=tuple(specs),
        out_specs=(P(rows), P("runs")),
        check_vma=False,
    )
```

```python
import functools
import math

import jax
import jax.numpy as jnp
from jax import lax
from jax.experimental import pallas as pl
from jax.experimental.pallas import tpu as pltpu
from jax.sharding import PartitionSpec as P

BF16, F32 = jnp.bfloat16, jnp.float32
VMEM = pl.BlockSpec(memory_space=pltpu.VMEM)
ANY = pl.BlockSpec(memory_space=pl.ANY)
SMEM = pl.BlockSpec(memory_space=pltpu.SMEM)
PARAMS = pltpu.CompilerParams(vmem_limit_bytes=16 * 2**20)
NT = (((1,), (1,)), ((), ()))
TN = (((0,), (0,)), ((), ()))
PARTS = 2
CHUNKS = 3
OUT_BLOCKS = 2


def in_hbm(*values):
    return [pltpu.with_memory_space_constraint(value, pltpu.HBM) for value in values]


def swap(value, axis, bit):
    pairs = [(source, source ^ (1 << bit)) for source in range(lax.axis_size(axis))]
    return lax.ppermute(value, axis, pairs)


def silu_slope(preact):
    sigmoid = jax.nn.sigmoid(preact)
    return sigmoid * (1.0 + preact * (1.0 - sigmoid))


def hop_bits(count):
    bits = count.bit_length() - 1
    return [*range(1, bits), 0]


def hop_order(count):
    hops = hop_bits(count)[::-1]
    return [sum(((i >> j) & 1) << bit for j, bit in enumerate(hops)) for i in range(count)]


def split_dot(weights, rows):
    high = weights.astype(BF16)
    low = (weights - high.astype(F32)).astype(BF16)
    return jnp.dot(high, rows, preferred_element_type=F32) + jnp.dot(
        low, rows, preferred_element_type=F32
    )


def gradient_kernel(
    features_hbm,
    aggregated_hbm,
    cotangent_hbm,
    self_hbm,
    neigh_hbm,
    inputs_ref,
    grad_ref,
    given_ref,
    cotangent,
    self_weight,
    neigh_weight,
    turned,
    sems,
):
    part_rows = cotangent.shape[0] // PARTS
    rows = part_rows // CHUNKS
    copies = []

    def fetch(source, target):
        copy = pltpu.make_async_copy(source, target, sems.at[len(copies)])
        copy.start()
        copies.append(copy)

    for p in range(PARTS):
        part = pl.ds(p * part_rows, part_rows)
        fetch(features_hbm.at[part], inputs_ref.at[0, part])
        if p == 0:
            fetch(self_hbm, self_weight)
            fetch(neigh_hbm, neigh_weight)
        fetch(aggregated_hbm.at[part], inputs_ref.at[1, part])
        fetch(cotangent_hbm.at[part], cotangent.at[part])
    other = 1 - lax.axis_index("hst")
    for p in range(PARTS):
        for copy in copies[:5] if p == 0 else copies[3 * p + 2 : 3 * p + 5]:
            copy.wait()
        for c in range(CHUNKS):
            part = pl.ds(p * part_rows + c * rows, rows)
            left, right = inputs_ref[0, part, :], inputs_ref[1, part, :]
            preact = jnp.dot(left, self_weight[...], preferred_element_type=F32) + jnp.dot(
                right, neigh_weight[...], preferred_element_type=F32
            )
            grad = (cotangent[part, :].astype(F32) * silu_slope(preact)).astype(BF16)
            grad_ref[part, :] = grad
            turned[:, part] = jnp.where(other == 0, left, right).T
    given_ref[...] = jnp.dot(
        turned[...], grad_ref[...], preferred_element_type=F32
    ).astype(BF16)


def kept_kernel(inputs_ref, grad_ref, after_ref, kept_ref):
    host = lax.axis_index("hst")
    kept_ref[...] = lax.dot_general(
        inputs_ref[host], grad_ref[...], TN, preferred_element_type=F32
    )


def outgoing_kernel(
    count_ref,
    grad_ref,
    weight_ref,
    source_ref,
    scale_ref,
    after_ref,
    neigh_ref,
    out_ref,
):
    peers, fan, cap = source_ref.shape
    me = lax.axis_index("dom")
    neigh = lax.dot_general(grad_ref[...], weight_ref[...], NT, preferred_element_type=F32)
    neigh = neigh.astype(BF16)
    neigh_ref[...] = neigh
    rows = neigh.shape[0]
    order = hop_order(peers)
    slot = lax.broadcasted_iota(jnp.int32, (fan, cap), 1)
    group = min(peers, 128 // cap)
    for first in range(0, peers, group):
        sources, scales = [], []
        for r in order[first : first + group]:
            q = jnp.bitwise_xor(me, r)
            live = slot < count_ref[0, q]
            sources.append(source_ref[q])
            scales.append(jnp.where(live, scale_ref[q], 0.0))
        sources = jnp.concatenate(sources, axis=1).T
        scales = jnp.concatenate(scales, axis=1).T
        slots = group * cap
        node = lax.broadcasted_iota(jnp.int32, (slots, rows), 1)
        select = jnp.zeros((slots, rows), F32)
        for k in range(fan):
            select += jnp.where(sources[:, k : k + 1] == node, scales[:, k : k + 1], 0.0)
        out_ref[pl.ds(first * cap, slots), :] = split_dot(select, neigh).astype(BF16)


def stale_kernel(
    version_ref, count_ref, stale_ref, weight_ref, source_ref, scale_ref, stay_ref, out_ref, same_ref
):
    chosen = stale_ref[version_ref[0]]
    neigh = lax.dot_general(chosen, weight_ref[...], NT, preferred_element_type=F32).astype(BF16)
    fan, slots = source_ref.shape
    live = lax.broadcasted_iota(jnp.int32, (1, slots), 1) < count_ref[0]
    stored = lax.broadcasted_iota(jnp.int32, (neigh.shape[0], slots), 0)
    select = jnp.zeros(stored.shape, F32)
    for k in range(fan):
        scale = jnp.where(live, scale_ref[pl.ds(k, 1), :], 0.0)
        select += jnp.where(source_ref[pl.ds(k, 1), :] == stored, scale, 0.0)
    out_ref[...] = split_dot(select.T, neigh).astype(BF16)


def local_kernel(
    source_ref,
    grad_ref,
    neigh_ref,
    weight_ref,
    tile_ref,
    stay_ref,
    base_ref,
    same_ref,
):
    blocks = base_ref.shape[0]
    tiles = tile_ref.shape[0]
    per_block = tiles // blocks
    for b in range(blocks):
        rows = pl.ds(b * 128, 128)
        base_ref[b] = lax.dot_general(
            grad_ref[rows, :], weight_ref[...], NT, preferred_element_type=F32
        )
    for b in range(blocks):
        neigh = neigh_ref[pl.ds(b * 128, 128), :]
        for t in range(b * per_block, (b + 1) * per_block):
            product = lax.dot_general(tile_ref[t], neigh, TN, preferred_element_type=F32)
            base_ref[source_ref[0, t]] += product


def finish_kernel(
    base_ref, fresh_ref, stale_ref, recv_ref, cross_ref, out_hbm, out, sems
):
    me = lax.axis_index("dom")
    blocks = base_ref.shape[0]
    peers, cap = recv_ref.shape
    targets = [recv_ref[pl.ds(jnp.bitwise_xor(me, o), 1), :] for o in hop_order(peers)]
    targets = jnp.concatenate(targets + [cross_ref[...]], axis=1)
    values = jnp.concatenate([fresh_ref[...], stale_ref[...]], axis=0)
    copies = []
    for b in range(blocks):
        node = b * 128 + lax.broadcasted_iota(jnp.int32, (128, targets.shape[1]), 0)
        hit = jnp.where(node == targets, 1.0, 0.0).astype(BF16)
        total = base_ref[b] + jnp.dot(hit, values, preferred_element_type=F32)
        out[pl.ds(b * 128, 128), :] = total.astype(BF16)
        if (b + 1) % OUT_BLOCKS == 0 or b + 1 == blocks:
            first = b // OUT_BLOCKS * OUT_BLOCKS
            part = pl.ds(first * 128, (b + 1 - first) * 128)
            copy = pltpu.make_async_copy(out.at[part], out_hbm.at[part], sems.at[len(copies)])
            copy.start()
            copies.append(copy)
    for copy in copies:
        copy.wait()


def sums_kernel(own_ref, across_ref, host_ref, last_ref, out_hbm, sems):
    quarter = own_ref.shape[0]
    host = lax.axis_index("hst")
    odd = jnp.bitwise_and(lax.axis_index("dom"), 1)
    here = pl.ds(pl.multiple_of(odd * quarter, quarter), quarter)
    there = pl.ds(pl.multiple_of((1 - odd) * quarter, quarter), quarter)
    copies = [
        pltpu.make_async_copy(own_ref, out_hbm.at[host, here], sems.at[0]),
        pltpu.make_async_copy(across_ref, out_hbm.at[host, there], sems.at[1]),
        pltpu.make_async_copy(host_ref, out_hbm.at[1 - host, here], sems.at[2]),
        pltpu.make_async_copy(last_ref, out_hbm.at[1 - host, there], sems.at[3]),
    ]
    for copy in copies:
        copy.start()
    for copy in copies:
        copy.wait()


def body(
    features,
    aggregated,
    cotangent,
    w_self,
    w_neigh,
    tile_values,
    tile_source,
    slot_source,
    slot_weight,
    send_count,
    recv_rows,
    stale_grad,
    version,
    cross_source,
    cross_weight,
    cross_count,
    cross_rows,
):
    row_count, dim = features.shape
    blocks = row_count // 128
    peers = lax.axis_size("dom")
    cap = slot_source.shape[2]
    bits = peers.bit_length() - 1
    me = lax.axis_index("dom")
    odd = (me & 1) == 1
    struct = jax.ShapeDtypeStruct

    inputs, pre_grad, given = pl.pallas_call(
        gradient_kernel,
        out_shape=(
            pltpu.VMEM((2, row_count, dim), BF16),
            pltpu.VMEM((row_count, dim), BF16),
            pltpu.VMEM((dim, dim), BF16),
        ),
        in_specs=[ANY] * 5,
        out_specs=(VMEM, VMEM, VMEM),
        scratch_shapes=[
            pltpu.VMEM((row_count, dim), BF16),
            pltpu.VMEM((dim, dim), BF16),
            pltpu.VMEM((dim, dim), BF16),
            pltpu.VMEM((dim, row_count), BF16),
            pltpu.SemaphoreType.DMA((2 + 3 * PARTS,)),
        ],
        compiler_params=PARAMS,
        name="gradients",
    )(*in_hbm(features, aggregated, cotangent, w_self, w_neigh))
    own = pl.pallas_call(
        kept_kernel,
        out_shape=pltpu.VMEM((dim, dim), F32),
        in_specs=[VMEM, VMEM, ANY],
        out_specs=VMEM,
        compiler_params=PARAMS,
        name="kept_sum",
    )(inputs, pre_grad, given)

    half = own + swap(given, "hst", 0).astype(F32)
    quarter = dim // 2
    low, high = half[:quarter], half[quarter:]
    kept, given = jnp.where(odd, high, low), jnp.where(odd, low, high).astype(BF16)
    kept = kept + swap(given, "dom", 0).astype(F32)

    neigh_grad, outgoing = pl.pallas_call(
        outgoing_kernel,
        out_shape=(struct((row_count, dim), BF16), struct((peers * cap, dim), BF16)),
        in_specs=[SMEM, VMEM, VMEM, VMEM, VMEM, ANY],
        out_specs=(VMEM, VMEM),
        compiler_params=PARAMS,
        name="outgoing",
    )(
        send_count,
        pre_grad,
        w_neigh,
        jnp.swapaxes(slot_source[0], 1, 2),
        jnp.swapaxes(slot_weight[0], 1, 2),
        given,
    )
    held = outgoing.reshape(1, peers * cap, dim)
    scale = 1.0 / math.sqrt(row_count * lax.axis_size("hst") * peers)
    for step, bit in enumerate(hop_bits(peers)):
        given = (kept if bit else kept * scale).astype(BF16)
        middle = held.shape[1] // 2
        stay, moved = held[:, :middle], held[:, middle:].reshape(-1, dim)
        arrived = swap(jnp.concatenate([given, moved], axis=0), "dom", bit)
        if step == 0:
            cross_out, stay = pl.pallas_call(
                stale_kernel,
                out_shape=(
                    struct((cross_source.shape[1], dim), BF16),
                    struct(stay.shape, stay.dtype),
                ),
                in_specs=[SMEM, SMEM, VMEM, VMEM, VMEM, VMEM, ANY],
                out_specs=(VMEM, ANY),
                input_output_aliases={6: 1},
                compiler_params=PARAMS,
                name="stale_rows",
            )(
                version,
                cross_count,
                stale_grad[0],
                w_neigh,
                cross_source[0].T,
                cross_weight[0].T,
                stay,
            )
        if step == 1:
            base, stay = pl.pallas_call(
                local_kernel,
                out_shape=(
                    struct((blocks, 128, dim), F32),
                    struct(stay.shape, stay.dtype),
                ),
                in_specs=[SMEM, VMEM, VMEM, VMEM, VMEM, ANY],
                out_specs=(VMEM, ANY),
                input_output_aliases={5: 1},
                compiler_params=PARAMS,
                name="local_term",
            )(tile_source, pre_grad, neigh_grad, w_self, tile_values[0], stay)
        other = arrived[:quarter]
        kept = given.astype(F32) + other.astype(F32)
        held = jnp.stack([stay, arrived[quarter:].reshape(stay.shape)], axis=1)
        held = held.reshape(-1, middle, dim)
    early = swap(jnp.concatenate([given, cross_out], axis=0), "hst", 0)
    stale_in = early[quarter:]
    last = swap(other, "hst", 0)
    sums = pl.pallas_call(
        sums_kernel,
        out_shape=struct((2, dim, dim), BF16),
        in_specs=[VMEM] * 4,
        out_specs=ANY,
        scratch_shapes=[pltpu.SemaphoreType.DMA((4,))],
        compiler_params=PARAMS,
        name="weight_grads",
    )(given, other, early[:quarter], last)

    out_rows = pl.pallas_call(
        finish_kernel,
        out_shape=struct((row_count, dim), BF16),
        in_specs=[VMEM] * 5,
        out_specs=ANY,
        scratch_shapes=[
            pltpu.VMEM((row_count, dim), BF16),
            pltpu.SemaphoreType.DMA((pl.cdiv(blocks, OUT_BLOCKS),)),
        ],
        compiler_params=PARAMS,
        name="finish",
    )(base, held.reshape(peers * cap, dim), stale_in, recv_rows[0], cross_rows)
    return (out_rows, sums)


def solution(mesh):
    rows = ("runs", "hst", "dom")
    specs = [P(rows)] * 17
    specs[3] = specs[4] = P()
    return jax.shard_map(
        body,
        mesh=mesh,
        in_specs=tuple(specs),
        out_specs=(P(rows), P("runs")),
        check_vma=False,
    )
```

```python
import functools
import math

import jax
import jax.numpy as jnp
from jax import lax
from jax.experimental import pallas as pl
from jax.experimental.pallas import tpu as pltpu
from jax.sharding import PartitionSpec as P

BF16, F32 = jnp.bfloat16, jnp.float32
VMEM = pl.BlockSpec(memory_space=pltpu.VMEM)
ANY = pl.BlockSpec(memory_space=pl.ANY)
SMEM = pl.BlockSpec(memory_space=pltpu.SMEM)
PARAMS = pltpu.CompilerParams(vmem_limit_bytes=16 * 2**20)
NT = (((1,), (1,)), ((), ()))
TN = (((0,), (0,)), ((), ()))
PARTS = 2
CHUNKS = 3
OUT_BLOCKS = 2


def in_hbm(*values):
    return [pltpu.with_memory_space_constraint(value, pltpu.HBM) for value in values]


def swap(value, axis, bit):
    pairs = [(source, source ^ (1 << bit)) for source in range(lax.axis_size(axis))]
    return lax.ppermute(value, axis, pairs)


def silu_slope(preact):
    sigmoid = jax.nn.sigmoid(preact)
    return sigmoid * (1.0 + preact * (1.0 - sigmoid))


def hop_bits(count):
    bits = count.bit_length() - 1
    return [*range(1, bits), 0]


def hop_order(count):
    hops = hop_bits(count)[::-1]
    return [sum(((i >> j) & 1) << bit for j, bit in enumerate(hops)) for i in range(count)]


def split_dot(weights, rows):
    high = weights.astype(BF16)
    low = (weights - high.astype(F32)).astype(BF16)
    return jnp.dot(high, rows, preferred_element_type=F32) + jnp.dot(
        low, rows, preferred_element_type=F32
    )


def gradient_kernel(
    features_hbm,
    aggregated_hbm,
    cotangent_hbm,
    self_hbm,
    neigh_hbm,
    inputs_ref,
    grad_ref,
    given_ref,
    cotangent,
    self_weight,
    neigh_weight,
    turned,
    sems,
):
    part_rows = cotangent.shape[0] // PARTS
    rows = part_rows // CHUNKS
    copies = []

    def fetch(source, target):
        copy = pltpu.make_async_copy(source, target, sems.at[len(copies)])
        copy.start()
        copies.append(copy)

    for p in range(PARTS):
        part = pl.ds(p * part_rows, part_rows)
        fetch(features_hbm.at[part], inputs_ref.at[0, part])
        if p == 0:
            fetch(self_hbm, self_weight)
            fetch(neigh_hbm, neigh_weight)
        fetch(aggregated_hbm.at[part], inputs_ref.at[1, part])
        fetch(cotangent_hbm.at[part], cotangent.at[part])
    other = 1 - lax.axis_index("hst")
    for p in range(PARTS):
        for copy in copies[:5] if p == 0 else copies[3 * p + 2 : 3 * p + 5]:
            copy.wait()
        for c in range(CHUNKS):
            part = pl.ds(p * part_rows + c * rows, rows)
            left, right = inputs_ref[0, part, :], inputs_ref[1, part, :]
            preact = jnp.dot(left, self_weight[...], preferred_element_type=F32) + jnp.dot(
                right, neigh_weight[...], preferred_element_type=F32
            )
            grad = (cotangent[part, :].astype(F32) * silu_slope(preact)).astype(BF16)
            grad_ref[part, :] = grad
            turned[:, part] = jnp.where(other == 0, left, right).T
    given_ref[...] = jnp.dot(
        turned[...], grad_ref[...], preferred_element_type=F32
    ).astype(BF16)


def kept_kernel(inputs_ref, grad_ref, after_ref, kept_ref):
    host = lax.axis_index("hst")
    kept_ref[...] = lax.dot_general(
        inputs_ref[host], grad_ref[...], TN, preferred_element_type=F32
    )


def outgoing_kernel(
    count_ref,
    grad_ref,
    weight_ref,
    source_ref,
    scale_ref,
    after_ref,
    neigh_ref,
    out_ref,
):
    peers, fan, cap = source_ref.shape
    me = lax.axis_index("dom")
    neigh = lax.dot_general(grad_ref[...], weight_ref[...], NT, preferred_element_type=F32)
    neigh = neigh.astype(BF16)
    neigh_ref[...] = neigh
    rows = neigh.shape[0]
    order = hop_order(peers)
    slot = lax.broadcasted_iota(jnp.int32, (fan, cap), 1)
    group = min(peers, 128 // cap)
    for first in range(0, peers, group):
        sources, scales = [], []
        for r in order[first : first + group]:
            q = jnp.bitwise_xor(me, r)
            live = slot < count_ref[0, q]
            sources.append(source_ref[q])
            scales.append(jnp.where(live, scale_ref[q], 0.0))
        sources = jnp.concatenate(sources, axis=1).T
        scales = jnp.concatenate(scales, axis=1).T
        slots = group * cap
        node = lax.broadcasted_iota(jnp.int32, (slots, rows), 1)
        select = jnp.zeros((slots, rows), F32)
        for k in range(fan):
            select += jnp.where(sources[:, k : k + 1] == node, scales[:, k : k + 1], 0.0)
        out_ref[pl.ds(first * cap, slots), :] = split_dot(select, neigh).astype(BF16)


def stale_kernel(
    version_ref, count_ref, stale_ref, weight_ref, source_ref, scale_ref, stay_ref, out_ref, same_ref
):
    chosen = stale_ref[version_ref[0]]
    neigh = lax.dot_general(chosen, weight_ref[...], NT, preferred_element_type=F32).astype(BF16)
    fan, slots = source_ref.shape
    live = lax.broadcasted_iota(jnp.int32, (1, slots), 1) < count_ref[0]
    stored = lax.broadcasted_iota(jnp.int32, (neigh.shape[0], slots), 0)
    select = jnp.zeros(stored.shape, F32)
    for k in range(fan):
        scale = jnp.where(live, scale_ref[pl.ds(k, 1), :], 0.0)
        select += jnp.where(source_ref[pl.ds(k, 1), :] == stored, scale, 0.0)
    out_ref[...] = split_dot(select.T, neigh).astype(BF16)


def local_kernel(
    source_ref,
    grad_ref,
    neigh_ref,
    weight_ref,
    tile_ref,
    stay_ref,
    base_ref,
    same_ref,
):
    blocks = base_ref.shape[0]
    tiles = tile_ref.shape[0]
    per_block = tiles // blocks
    for b in range(blocks):
        rows = pl.ds(b * 128, 128)
        base_ref[b] = lax.dot_general(
            grad_ref[rows, :], weight_ref[...], NT, preferred_element_type=F32
        )
    for b in range(blocks):
        neigh = neigh_ref[pl.ds(b * 128, 128), :]
        for t in range(b * per_block, (b + 1) * per_block):
            product = lax.dot_general(tile_ref[t], neigh, TN, preferred_element_type=F32)
            base_ref[source_ref[0, t]] += product


def quarters(size):
    odd = jnp.bitwise_and(lax.axis_index("dom"), 1)
    return [pl.ds(pl.multiple_of(i * size, size), size) for i in (odd, 1 - odd)]


def finish_kernel(
    base_ref,
    fresh_ref,
    stale_ref,
    recv_ref,
    cross_ref,
    own_ref,
    across_ref,
    host_ref,
    out_hbm,
    sums_hbm,
    out,
    sems,
):
    me = lax.axis_index("dom")
    blocks = base_ref.shape[0]
    peers, cap = recv_ref.shape
    targets = [recv_ref[pl.ds(jnp.bitwise_xor(me, o), 1), :] for o in hop_order(peers)]
    targets = jnp.concatenate(targets + [cross_ref[...]], axis=1)
    values = jnp.concatenate([fresh_ref[...], stale_ref[...]], axis=0)
    host = lax.axis_index("hst")
    here, there = quarters(own_ref.shape[0])
    copies = [
        pltpu.make_async_copy(own_ref, sums_hbm.at[host, here], sems.at[0]),
        pltpu.make_async_copy(across_ref, sums_hbm.at[host, there], sems.at[1]),
        pltpu.make_async_copy(host_ref, sums_hbm.at[1 - host, here], sems.at[2]),
    ]
    for copy in copies:
        copy.start()
    for b in range(blocks):
        node = b * 128 + lax.broadcasted_iota(jnp.int32, (128, targets.shape[1]), 0)
        hit = jnp.where(node == targets, 1.0, 0.0).astype(BF16)
        total = base_ref[b] + jnp.dot(hit, values, preferred_element_type=F32)
        out[pl.ds(b * 128, 128), :] = total.astype(BF16)
        if (b + 1) % OUT_BLOCKS == 0 or b + 1 == blocks:
            first = b // OUT_BLOCKS * OUT_BLOCKS
            part = pl.ds(first * 128, (b + 1 - first) * 128)
            copy = pltpu.make_async_copy(out.at[part], out_hbm.at[part], sems.at[len(copies)])
            copy.start()
            copies.append(copy)
    for copy in copies:
        copy.wait()


def last_kernel(last_ref, sums_in, sums_hbm, sem):
    here, there = quarters(last_ref.shape[0])
    host = lax.axis_index("hst")
    copy = pltpu.make_async_copy(last_ref, sums_hbm.at[1 - host, there], sem)
    copy.start()
    copy.wait()


def body(
    features,
    aggregated,
    cotangent,
    w_self,
    w_neigh,
    tile_values,
    tile_source,
    slot_source,
    slot_weight,
    send_count,
    recv_rows,
    stale_grad,
    version,
    cross_source,
    cross_weight,
    cross_count,
    cross_rows,
):
    row_count, dim = features.shape
    blocks = row_count // 128
    peers = lax.axis_size("dom")
    cap = slot_source.shape[2]
    bits = peers.bit_length() - 1
    me = lax.axis_index("dom")
    odd = (me & 1) == 1
    struct = jax.ShapeDtypeStruct

    inputs, pre_grad, given = pl.pallas_call(
        gradient_kernel,
        out_shape=(
            pltpu.VMEM((2, row_count, dim), BF16),
            pltpu.VMEM((row_count, dim), BF16),
            pltpu.VMEM((dim, dim), BF16),
        ),
        in_specs=[ANY] * 5,
        out_specs=(VMEM, VMEM, VMEM),
        scratch_shapes=[
            pltpu.VMEM((row_count, dim), BF16),
            pltpu.VMEM((dim, dim), BF16),
            pltpu.VMEM((dim, dim), BF16),
            pltpu.VMEM((dim, row_count), BF16),
            pltpu.SemaphoreType.DMA((2 + 3 * PARTS,)),
        ],
        compiler_params=PARAMS,
        name="gradients",
    )(*in_hbm(features, aggregated, cotangent, w_self, w_neigh))
    own = pl.pallas_call(
        kept_kernel,
        out_shape=pltpu.VMEM((dim, dim), F32),
        in_specs=[VMEM, VMEM, ANY],
        out_specs=VMEM,
        compiler_params=PARAMS,
        name="kept_sum",
    )(inputs, pre_grad, given)

    half = own + swap(given, "hst", 0).astype(F32)
    quarter = dim // 2
    low, high = half[:quarter], half[quarter:]
    kept, given = jnp.where(odd, high, low), jnp.where(odd, low, high).astype(BF16)
    kept = kept + swap(given, "dom", 0).astype(F32)

    neigh_grad, outgoing = pl.pallas_call(
        outgoing_kernel,
        out_shape=(struct((row_count, dim), BF16), struct((peers * cap, dim), BF16)),
        in_specs=[SMEM, VMEM, VMEM, VMEM, VMEM, ANY],
        out_specs=(VMEM, VMEM),
        compiler_params=PARAMS,
        name="outgoing",
    )(
        send_count,
        pre_grad,
        w_neigh,
        jnp.swapaxes(slot_source[0], 1, 2),
        jnp.swapaxes(slot_weight[0], 1, 2),
        given,
    )
    held = outgoing.reshape(1, peers * cap, dim)
    scale = 1.0 / math.sqrt(row_count * lax.axis_size("hst") * peers)
    for step, bit in enumerate(hop_bits(peers)):
        given = (kept if bit else kept * scale).astype(BF16)
        middle = held.shape[1] // 2
        stay, moved = held[:, :middle], held[:, middle:].reshape(-1, dim)
        arrived = swap(jnp.concatenate([given, moved], axis=0), "dom", bit)
        if step == 0:
            cross_out, stay = pl.pallas_call(
                stale_kernel,
                out_shape=(
                    struct((cross_source.shape[1], dim), BF16),
                    struct(stay.shape, stay.dtype),
                ),
                in_specs=[SMEM, SMEM, VMEM, VMEM, VMEM, VMEM, ANY],
                out_specs=(VMEM, ANY),
                input_output_aliases={6: 1},
                compiler_params=PARAMS,
                name="stale_rows",
            )(
                version,
                cross_count,
                stale_grad[0],
                w_neigh,
                cross_source[0].T,
                cross_weight[0].T,
                stay,
            )
        if step == 1:
            base, stay = pl.pallas_call(
                local_kernel,
                out_shape=(
                    struct((blocks, 128, dim), F32),
                    struct(stay.shape, stay.dtype),
                ),
                in_specs=[SMEM, VMEM, VMEM, VMEM, VMEM, ANY],
                out_specs=(VMEM, ANY),
                input_output_aliases={5: 1},
                compiler_params=PARAMS,
                name="local_term",
            )(tile_source, pre_grad, neigh_grad, w_self, tile_values[0], stay)
        other = arrived[:quarter]
        kept = given.astype(F32) + other.astype(F32)
        held = jnp.stack([stay, arrived[quarter:].reshape(stay.shape)], axis=1)
        held = held.reshape(-1, middle, dim)
    early = swap(jnp.concatenate([given, cross_out], axis=0), "hst", 0)
    stale_in = early[quarter:]
    last = swap(other, "hst", 0)
    out_rows, sums = pl.pallas_call(
        finish_kernel,
        out_shape=(struct((row_count, dim), BF16), struct((2, dim, dim), BF16)),
        in_specs=[VMEM] * 8,
        out_specs=(ANY, ANY),
        scratch_shapes=[
            pltpu.VMEM((row_count, dim), BF16),
            pltpu.SemaphoreType.DMA((3 + pl.cdiv(blocks, OUT_BLOCKS),)),
        ],
        compiler_params=PARAMS,
        name="finish",
    )(
        base,
        held.reshape(peers * cap, dim),
        stale_in,
        recv_rows[0],
        cross_rows,
        given,
        other,
        early[:quarter],
    )
    sums = pl.pallas_call(
        last_kernel,
        out_shape=struct((2, dim, dim), BF16),
        in_specs=[VMEM, ANY],
        out_specs=ANY,
        input_output_aliases={1: 0},
        scratch_shapes=[pltpu.SemaphoreType.DMA],
        compiler_params=PARAMS,
        name="weight_grads",
    )(last, sums)
    return (out_rows, sums)


def solution(mesh):
    rows = ("runs", "hst", "dom")
    specs = [P(rows)] * 17
    specs[3] = specs[4] = P()
    return jax.shard_map(
        body,
        mesh=mesh,
        in_specs=tuple(specs),
        out_specs=(P(rows), P("runs")),
        check_vma=False,
    )
```

```python
import functools
import math

import jax
import jax.numpy as jnp
from jax import lax
from jax.experimental import pallas as pl
from jax.experimental.pallas import tpu as pltpu
from jax.sharding import PartitionSpec as P

BF16, F32 = jnp.bfloat16, jnp.float32
VMEM = pl.BlockSpec(memory_space=pltpu.VMEM)
ANY = pl.BlockSpec(memory_space=pl.ANY)
SMEM = pl.BlockSpec(memory_space=pltpu.SMEM)
PARAMS = pltpu.CompilerParams(vmem_limit_bytes=16 * 2**20)
NT = (((1,), (1,)), ((), ()))
TN = (((0,), (0,)), ((), ()))
PARTS = 2
CHUNKS = 3
OUT_BLOCKS = 2


def in_hbm(*values):
    return [pltpu.with_memory_space_constraint(value, pltpu.HBM) for value in values]


def swap(value, axis, bit):
    pairs = [(source, source ^ (1 << bit)) for source in range(lax.axis_size(axis))]
    return lax.ppermute(value, axis, pairs)


def silu_slope(preact):
    sigmoid = jax.nn.sigmoid(preact)
    return sigmoid * (1.0 + preact * (1.0 - sigmoid))


def hop_bits(count):
    bits = count.bit_length() - 1
    return [*range(1, bits), 0]


def hop_order(count, first_hop_fastest=False):
    hops = hop_bits(count) if first_hop_fastest else hop_bits(count)[::-1]
    return [sum(((i >> j) & 1) << bit for j, bit in enumerate(hops)) for i in range(count)]


def split_dot(weights, rows):
    high = weights.astype(BF16)
    low = (weights - high.astype(F32)).astype(BF16)
    return jnp.dot(high, rows, preferred_element_type=F32) + jnp.dot(
        low, rows, preferred_element_type=F32
    )


def gradient_kernel(
    features_hbm,
    aggregated_hbm,
    cotangent_hbm,
    self_hbm,
    neigh_hbm,
    inputs_ref,
    grad_ref,
    given_ref,
    cotangent,
    self_weight,
    neigh_weight,
    turned,
    sems,
):
    part_rows = cotangent.shape[0] // PARTS
    rows = part_rows // CHUNKS
    copies = []

    def fetch(source, target):
        copy = pltpu.make_async_copy(source, target, sems.at[len(copies)])
        copy.start()
        copies.append(copy)

    for p in range(PARTS):
        part = pl.ds(p * part_rows, part_rows)
        fetch(features_hbm.at[part], inputs_ref.at[0, part])
        if p == 0:
            fetch(self_hbm, self_weight)
            fetch(neigh_hbm, neigh_weight)
        fetch(aggregated_hbm.at[part], inputs_ref.at[1, part])
        fetch(cotangent_hbm.at[part], cotangent.at[part])
    other = 1 - lax.axis_index("hst")
    for p in range(PARTS):
        for copy in copies[:5] if p == 0 else copies[3 * p + 2 : 3 * p + 5]:
            copy.wait()
        for c in range(CHUNKS):
            part = pl.ds(p * part_rows + c * rows, rows)
            left, right = inputs_ref[0, part, :], inputs_ref[1, part, :]
            preact = jnp.dot(left, self_weight[...], preferred_element_type=F32) + jnp.dot(
                right, neigh_weight[...], preferred_element_type=F32
            )
            grad = (cotangent[part, :].astype(F32) * silu_slope(preact)).astype(BF16)
            grad_ref[part, :] = grad
            turned[:, part] = jnp.where(other == 0, left, right).T
    given_ref[...] = jnp.dot(
        turned[...], grad_ref[...], preferred_element_type=F32
    ).astype(BF16)


def kept_kernel(inputs_ref, grad_ref, after_ref, kept_ref):
    host = lax.axis_index("hst")
    kept_ref[...] = lax.dot_general(
        inputs_ref[host], grad_ref[...], TN, preferred_element_type=F32
    )


def outgoing_kernel(
    count_ref,
    grad_ref,
    weight_ref,
    source_ref,
    scale_ref,
    after_ref,
    neigh_ref,
    out_ref,
):
    peers, fan, cap = source_ref.shape
    me = lax.axis_index("dom")
    neigh = lax.dot_general(grad_ref[...], weight_ref[...], NT, preferred_element_type=F32)
    neigh = neigh.astype(BF16)
    neigh_ref[...] = neigh
    rows = neigh.shape[0]
    order = hop_order(peers)
    slot = lax.broadcasted_iota(jnp.int32, (fan, cap), 1)
    group = min(peers, 128 // cap)
    for first in range(0, peers, group):
        sources, scales = [], []
        for r in order[first : first + group]:
            q = jnp.bitwise_xor(me, r)
            live = slot < count_ref[0, q]
            sources.append(source_ref[q])
            scales.append(jnp.where(live, scale_ref[q], 0.0))
        sources = jnp.concatenate(sources, axis=1).T
        scales = jnp.concatenate(scales, axis=1).T
        slots = group * cap
        node = lax.broadcasted_iota(jnp.int32, (slots, rows), 1)
        select = jnp.zeros((slots, rows), F32)
        for k in range(fan):
            select += jnp.where(sources[:, k : k + 1] == node, scales[:, k : k + 1], 0.0)
        out_ref[pl.ds(first * cap, slots), :] = split_dot(select, neigh).astype(BF16)


def stale_kernel(
    version_ref, count_ref, stale_ref, weight_ref, source_ref, scale_ref, stay_ref, out_ref, same_ref
):
    chosen = stale_ref[version_ref[0]]
    neigh = lax.dot_general(chosen, weight_ref[...], NT, preferred_element_type=F32).astype(BF16)
    fan, slots = source_ref.shape
    live = lax.broadcasted_iota(jnp.int32, (1, slots), 1) < count_ref[0]
    stored = lax.broadcasted_iota(jnp.int32, (neigh.shape[0], slots), 0)
    select = jnp.zeros(stored.shape, F32)
    for k in range(fan):
        scale = jnp.where(live, scale_ref[pl.ds(k, 1), :], 0.0)
        select += jnp.where(source_ref[pl.ds(k, 1), :] == stored, scale, 0.0)
    out_ref[...] = split_dot(select.T, neigh).astype(BF16)


def local_kernel(
    source_ref,
    grad_ref,
    neigh_ref,
    weight_ref,
    tile_ref,
    stay_ref,
    base_ref,
    same_ref,
):
    blocks = base_ref.shape[0]
    tiles = tile_ref.shape[0]
    per_block = tiles // blocks
    for b in range(blocks):
        rows = pl.ds(b * 128, 128)
        base_ref[b] = lax.dot_general(
            grad_ref[rows, :], weight_ref[...], NT, preferred_element_type=F32
        )
    for b in range(blocks):
        neigh = neigh_ref[pl.ds(b * 128, 128), :]
        for t in range(b * per_block, (b + 1) * per_block):
            product = lax.dot_general(tile_ref[t], neigh, TN, preferred_element_type=F32)
            base_ref[source_ref[0, t]] += product


def quarters(size):
    odd = jnp.bitwise_and(lax.axis_index("dom"), 1)
    return [pl.ds(pl.multiple_of(i * size, size), size) for i in (odd, 1 - odd)]


def finish_kernel(
    base_ref,
    fresh_ref,
    stale_ref,
    recv_ref,
    cross_ref,
    own_ref,
    across_ref,
    host_ref,
    out_hbm,
    sums_hbm,
    out,
    sems,
):
    me = lax.axis_index("dom")
    blocks = base_ref.shape[0]
    peers, cap = recv_ref.shape
    targets = [recv_ref[pl.ds(jnp.bitwise_xor(me, o), 1), :] for o in hop_order(peers, True)]
    targets = jnp.concatenate(targets + [cross_ref[...]], axis=1)
    values = jnp.concatenate([fresh_ref[...], stale_ref[...]], axis=0)
    host = lax.axis_index("hst")
    here, there = quarters(own_ref.shape[0])
    copies = [
        pltpu.make_async_copy(own_ref, sums_hbm.at[host, here], sems.at[0]),
        pltpu.make_async_copy(across_ref, sums_hbm.at[host, there], sems.at[1]),
        pltpu.make_async_copy(host_ref, sums_hbm.at[1 - host, here], sems.at[2]),
    ]
    for copy in copies:
        copy.start()
    for b in range(blocks):
        node = b * 128 + lax.broadcasted_iota(jnp.int32, (128, targets.shape[1]), 0)
        hit = jnp.where(node == targets, 1.0, 0.0).astype(BF16)
        total = base_ref[b] + jnp.dot(hit, values, preferred_element_type=F32)
        out[pl.ds(b * 128, 128), :] = total.astype(BF16)
        if (b + 1) % OUT_BLOCKS == 0 or b + 1 == blocks:
            first = b // OUT_BLOCKS * OUT_BLOCKS
            part = pl.ds(first * 128, (b + 1 - first) * 128)
            copy = pltpu.make_async_copy(out.at[part], out_hbm.at[part], sems.at[len(copies)])
            copy.start()
            copies.append(copy)
    for copy in copies:
        copy.wait()


def last_kernel(last_ref, sums_in, sums_hbm, sem):
    here, there = quarters(last_ref.shape[0])
    host = lax.axis_index("hst")
    copy = pltpu.make_async_copy(last_ref, sums_hbm.at[1 - host, there], sem)
    copy.start()
    copy.wait()


def body(
    features,
    aggregated,
    cotangent,
    w_self,
    w_neigh,
    tile_values,
    tile_source,
    slot_source,
    slot_weight,
    send_count,
    recv_rows,
    stale_grad,
    version,
    cross_source,
    cross_weight,
    cross_count,
    cross_rows,
):
    row_count, dim = features.shape
    blocks = row_count // 128
    peers = lax.axis_size("dom")
    cap = slot_source.shape[2]
    bits = peers.bit_length() - 1
    me = lax.axis_index("dom")
    odd = (me & 1) == 1
    struct = jax.ShapeDtypeStruct

    inputs, pre_grad, given = pl.pallas_call(
        gradient_kernel,
        out_shape=(
            pltpu.VMEM((2, row_count, dim), BF16),
            pltpu.VMEM((row_count, dim), BF16),
            pltpu.VMEM((dim, dim), BF16),
        ),
        in_specs=[ANY] * 5,
        out_specs=(VMEM, VMEM, VMEM),
        scratch_shapes=[
            pltpu.VMEM((row_count, dim), BF16),
            pltpu.VMEM((dim, dim), BF16),
            pltpu.VMEM((dim, dim), BF16),
            pltpu.VMEM((dim, row_count), BF16),
            pltpu.SemaphoreType.DMA((2 + 3 * PARTS,)),
        ],
        compiler_params=PARAMS,
        name="gradients",
    )(*in_hbm(features, aggregated, cotangent, w_self, w_neigh))
    own = pl.pallas_call(
        kept_kernel,
        out_shape=pltpu.VMEM((dim, dim), F32),
        in_specs=[VMEM, VMEM, ANY],
        out_specs=VMEM,
        compiler_params=PARAMS,
        name="kept_sum",
    )(inputs, pre_grad, given)

    half = own + swap(given, "hst", 0).astype(F32)
    quarter = dim // 2
    low, high = half[:quarter], half[quarter:]
    kept, given = jnp.where(odd, high, low), jnp.where(odd, low, high).astype(BF16)
    kept = kept + swap(given, "dom", 0).astype(F32)

    neigh_grad, outgoing = pl.pallas_call(
        outgoing_kernel,
        out_shape=(struct((row_count, dim), BF16), struct((peers * cap, dim), BF16)),
        in_specs=[SMEM, VMEM, VMEM, VMEM, VMEM, ANY],
        out_specs=(VMEM, VMEM),
        compiler_params=PARAMS,
        name="outgoing",
    )(
        send_count,
        pre_grad,
        w_neigh,
        jnp.swapaxes(slot_source[0], 1, 2),
        jnp.swapaxes(slot_weight[0], 1, 2),
        given,
    )
    held = outgoing.reshape(1, peers * cap, dim)
    scale = 1.0 / math.sqrt(row_count * lax.axis_size("hst") * peers)
    for step, bit in enumerate(hop_bits(peers)):
        given = (kept if bit else kept * scale).astype(BF16)
        middle = held.shape[1] // 2
        stay, moved = held[:, :middle], held[:, middle:].reshape(-1, dim)
        arrived = swap(jnp.concatenate([given, moved], axis=0), "dom", bit)
        if step == 0:
            cross_out, stay = pl.pallas_call(
                stale_kernel,
                out_shape=(
                    struct((cross_source.shape[1], dim), BF16),
                    struct(stay.shape, stay.dtype),
                ),
                in_specs=[SMEM, SMEM, VMEM, VMEM, VMEM, VMEM, ANY],
                out_specs=(VMEM, ANY),
                input_output_aliases={6: 1},
                compiler_params=PARAMS,
                name="stale_rows",
            )(
                version,
                cross_count,
                stale_grad[0],
                w_neigh,
                cross_source[0].T,
                cross_weight[0].T,
                stay,
            )
        if step == 1:
            base, stay = pl.pallas_call(
                local_kernel,
                out_shape=(
                    struct((blocks, 128, dim), F32),
                    struct(stay.shape, stay.dtype),
                ),
                in_specs=[SMEM, VMEM, VMEM, VMEM, VMEM, ANY],
                out_specs=(VMEM, ANY),
                input_output_aliases={5: 1},
                compiler_params=PARAMS,
                name="local_term",
            )(tile_source, pre_grad, neigh_grad, w_self, tile_values[0], stay)
        other = arrived[:quarter]
        kept = given.astype(F32) + other.astype(F32)
        held = jnp.concatenate([stay, arrived[quarter:].reshape(stay.shape)], axis=0)
    early = swap(jnp.concatenate([given, cross_out], axis=0), "hst", 0)
    stale_in = early[quarter:]
    last = swap(other, "hst", 0)
    out_rows, sums = pl.pallas_call(
        finish_kernel,
        out_shape=(struct((row_count, dim), BF16), struct((2, dim, dim), BF16)),
        in_specs=[VMEM] * 8,
        out_specs=(ANY, ANY),
        scratch_shapes=[
            pltpu.VMEM((row_count, dim), BF16),
            pltpu.SemaphoreType.DMA((3 + pl.cdiv(blocks, OUT_BLOCKS),)),
        ],
        compiler_params=PARAMS,
        name="finish",
    )(
        base,
        held.reshape(peers * cap, dim),
        stale_in,
        recv_rows[0],
        cross_rows,
        given,
        other,
        early[:quarter],
    )
    sums = pl.pallas_call(
        last_kernel,
        out_shape=struct((2, dim, dim), BF16),
        in_specs=[VMEM, ANY],
        out_specs=ANY,
        input_output_aliases={1: 0},
        scratch_shapes=[pltpu.SemaphoreType.DMA],
        compiler_params=PARAMS,
        name="weight_grads",
    )(last, sums)
    return (out_rows, sums)


def solution(mesh):
    rows = ("runs", "hst", "dom")
    specs = [P(rows)] * 17
    specs[3] = specs[4] = P()
    return jax.shard_map(
        body,
        mesh=mesh,
        in_specs=tuple(specs),
        out_specs=(P(rows), P("runs")),
        check_vma=False,
    )
```

```python
import functools
import math

import jax
import jax.numpy as jnp
from jax import lax
from jax.experimental import pallas as pl
from jax.experimental.pallas import tpu as pltpu
from jax.sharding import PartitionSpec as P

BF16, F32 = jnp.bfloat16, jnp.float32
VMEM = pl.BlockSpec(memory_space=pltpu.VMEM)
ANY = pl.BlockSpec(memory_space=pl.ANY)
SMEM = pl.BlockSpec(memory_space=pltpu.SMEM)
PARAMS = pltpu.CompilerParams(vmem_limit_bytes=16 * 2**20)
NT = (((1,), (1,)), ((), ()))
TN = (((0,), (0,)), ((), ()))
PARTS = 2
CHUNKS = 3
OUT_BLOCKS = 2


def in_hbm(*values):
    return [pltpu.with_memory_space_constraint(value, pltpu.HBM) for value in values]


def swap(value, axis, bit):
    pairs = [(source, source ^ (1 << bit)) for source in range(lax.axis_size(axis))]
    return lax.ppermute(value, axis, pairs)


def silu_slope(preact):
    sigmoid = jax.nn.sigmoid(preact)
    return sigmoid * (1.0 + preact * (1.0 - sigmoid))


def hop_bits(count):
    bits = count.bit_length() - 1
    return [*range(1, bits), 0]


def hop_order(count):
    hops = hop_bits(count)[::-1]
    return [sum(((i >> j) & 1) << bit for j, bit in enumerate(hops)) for i in range(count)]


def split_dot(weights, rows):
    high = weights.astype(BF16)
    low = (weights - high.astype(F32)).astype(BF16)
    return jnp.dot(high, rows, preferred_element_type=F32) + jnp.dot(
        low, rows, preferred_element_type=F32
    )


def gradient_kernel(
    features_hbm,
    aggregated_hbm,
    cotangent_hbm,
    self_hbm,
    neigh_hbm,
    inputs_ref,
    grad_ref,
    given_ref,
    cotangent,
    self_weight,
    neigh_weight,
    turned,
    sems,
):
    part_rows = cotangent.shape[0] // PARTS
    rows = part_rows // CHUNKS
    copies = []

    def fetch(source, target):
        copy = pltpu.make_async_copy(source, target, sems.at[len(copies)])
        copy.start()
        copies.append(copy)

    for p in range(PARTS):
        part = pl.ds(p * part_rows, part_rows)
        fetch(features_hbm.at[part], inputs_ref.at[0, part])
        if p == 0:
            fetch(self_hbm, self_weight)
            fetch(neigh_hbm, neigh_weight)
        fetch(aggregated_hbm.at[part], inputs_ref.at[1, part])
        fetch(cotangent_hbm.at[part], cotangent.at[part])
    other = 1 - lax.axis_index("hst")
    for p in range(PARTS):
        for copy in copies[:5] if p == 0 else copies[3 * p + 2 : 3 * p + 5]:
            copy.wait()
        for c in range(CHUNKS):
            part = pl.ds(p * part_rows + c * rows, rows)
            left, right = inputs_ref[0, part, :], inputs_ref[1, part, :]
            preact = jnp.dot(left, self_weight[...], preferred_element_type=F32) + jnp.dot(
                right, neigh_weight[...], preferred_element_type=F32
            )
            grad = (cotangent[part, :].astype(F32) * silu_slope(preact)).astype(BF16)
            grad_ref[part, :] = grad
            turned[:, part] = jnp.where(other == 0, left, right).T
    given_ref[...] = jnp.dot(
        turned[...], grad_ref[...], preferred_element_type=F32
    ).astype(BF16)


def kept_kernel(inputs_ref, grad_ref, after_ref, kept_ref):
    host = lax.axis_index("hst")
    kept_ref[...] = lax.dot_general(
        inputs_ref[host], grad_ref[...], TN, preferred_element_type=F32
    )


def outgoing_kernel(
    count_ref,
    grad_ref,
    weight_ref,
    source_ref,
    scale_ref,
    after_ref,
    neigh_ref,
    out_ref,
):
    peers, fan, cap = source_ref.shape
    me = lax.axis_index("dom")
    neigh = lax.dot_general(grad_ref[...], weight_ref[...], NT, preferred_element_type=F32)
    neigh = neigh.astype(BF16)
    neigh_ref[...] = neigh
    rows = neigh.shape[0]
    order = hop_order(peers)
    slot = lax.broadcasted_iota(jnp.int32, (fan, cap), 1)
    group = min(peers, 128 // cap)
    for first in range(0, peers, group):
        sources, scales = [], []
        for r in order[first : first + group]:
            q = jnp.bitwise_xor(me, r)
            live = slot < count_ref[0, q]
            sources.append(source_ref[q])
            scales.append(jnp.where(live, scale_ref[q], 0.0))
        sources = jnp.concatenate(sources, axis=1).T
        scales = jnp.concatenate(scales, axis=1).T
        slots = group * cap
        node = lax.broadcasted_iota(jnp.int32, (slots, rows), 1)
        select = jnp.zeros((slots, rows), F32)
        for k in range(fan):
            select += jnp.where(sources[:, k : k + 1] == node, scales[:, k : k + 1], 0.0)
        out_ref[pl.ds(first * cap, slots), :] = split_dot(select, neigh).astype(BF16)


def stale_kernel(
    version_ref, count_ref, stale_ref, weight_ref, source_ref, scale_ref, stay_ref, out_ref, same_ref
):
    chosen = stale_ref[version_ref[0]]
    neigh = lax.dot_general(chosen, weight_ref[...], NT, preferred_element_type=F32).astype(BF16)
    fan, slots = source_ref.shape
    live = lax.broadcasted_iota(jnp.int32, (1, slots), 1) < count_ref[0]
    stored = lax.broadcasted_iota(jnp.int32, (neigh.shape[0], slots), 0)
    select = jnp.zeros(stored.shape, F32)
    for k in range(fan):
        scale = jnp.where(live, scale_ref[pl.ds(k, 1), :], 0.0)
        select += jnp.where(source_ref[pl.ds(k, 1), :] == stored, scale, 0.0)
    out_ref[...] = split_dot(select.T, neigh).astype(BF16)


def local_kernel(
    source_ref,
    grad_ref,
    neigh_ref,
    weight_ref,
    tile_ref,
    recv_ref,
    cross_ref,
    stay_ref,
    base_ref,
    hit_ref,
    same_ref,
):
    blocks = base_ref.shape[0]
    tiles = tile_ref.shape[0]
    per_block = tiles // blocks
    for b in range(blocks):
        rows = pl.ds(b * 128, 128)
        base_ref[b] = lax.dot_general(
            grad_ref[rows, :], weight_ref[...], NT, preferred_element_type=F32
        )
    for b in range(blocks):
        neigh = neigh_ref[pl.ds(b * 128, 128), :]
        for t in range(b * per_block, (b + 1) * per_block):
            product = lax.dot_general(tile_ref[t], neigh, TN, preferred_element_type=F32)
            base_ref[source_ref[0, t]] += product
    me = lax.axis_index("dom")
    targets = [recv_ref[pl.ds(jnp.bitwise_xor(me, o), 1), :] for o in hop_order(recv_ref.shape[0])]
    targets = jnp.concatenate(targets + [cross_ref[...]], axis=1)
    for b in range(blocks):
        node = b * 128 + lax.broadcasted_iota(jnp.int32, (128, targets.shape[1]), 0)
        hit_ref[pl.ds(b * 128, 128), :] = jnp.where(node == targets, 1.0, 0.0).astype(BF16)


def quarters(size):
    odd = jnp.bitwise_and(lax.axis_index("dom"), 1)
    return [pl.ds(pl.multiple_of(i * size, size), size) for i in (odd, 1 - odd)]


def finish_kernel(
    base_ref,
    fresh_ref,
    stale_ref,
    hit_ref,
    own_ref,
    across_ref,
    host_ref,
    out_hbm,
    sums_hbm,
    out,
    sems,
):
    blocks = base_ref.shape[0]
    values = jnp.concatenate([fresh_ref[...], stale_ref[...]], axis=0)
    host = lax.axis_index("hst")
    here, there = quarters(own_ref.shape[0])
    copies = [
        pltpu.make_async_copy(own_ref, sums_hbm.at[host, here], sems.at[0]),
        pltpu.make_async_copy(across_ref, sums_hbm.at[host, there], sems.at[1]),
        pltpu.make_async_copy(host_ref, sums_hbm.at[1 - host, here], sems.at[2]),
    ]
    for copy in copies:
        copy.start()
    for b in range(blocks):
        hit = hit_ref[pl.ds(b * 128, 128), :]
        total = base_ref[b] + jnp.dot(hit, values, preferred_element_type=F32)
        out[pl.ds(b * 128, 128), :] = total.astype(BF16)
        if (b + 1) % OUT_BLOCKS == 0 or b + 1 == blocks:
            first = b // OUT_BLOCKS * OUT_BLOCKS
            part = pl.ds(first * 128, (b + 1 - first) * 128)
            copy = pltpu.make_async_copy(out.at[part], out_hbm.at[part], sems.at[len(copies)])
            copy.start()
            copies.append(copy)
    for copy in copies:
        copy.wait()


def last_kernel(last_ref, sums_in, sums_hbm, sem):
    here, there = quarters(last_ref.shape[0])
    host = lax.axis_index("hst")
    copy = pltpu.make_async_copy(last_ref, sums_hbm.at[1 - host, there], sem)
    copy.start()
    copy.wait()


def body(
    features,
    aggregated,
    cotangent,
    w_self,
    w_neigh,
    tile_values,
    tile_source,
    slot_source,
    slot_weight,
    send_count,
    recv_rows,
    stale_grad,
    version,
    cross_source,
    cross_weight,
    cross_count,
    cross_rows,
):
    row_count, dim = features.shape
    blocks = row_count // 128
    peers = lax.axis_size("dom")
    cap = slot_source.shape[2]
    bits = peers.bit_length() - 1
    me = lax.axis_index("dom")
    odd = (me & 1) == 1
    struct = jax.ShapeDtypeStruct

    inputs, pre_grad, given = pl.pallas_call(
        gradient_kernel,
        out_shape=(
            pltpu.VMEM((2, row_count, dim), BF16),
            pltpu.VMEM((row_count, dim), BF16),
            pltpu.VMEM((dim, dim), BF16),
        ),
        in_specs=[ANY] * 5,
        out_specs=(VMEM, VMEM, VMEM),
        scratch_shapes=[
            pltpu.VMEM((row_count, dim), BF16),
            pltpu.VMEM((dim, dim), BF16),
            pltpu.VMEM((dim, dim), BF16),
            pltpu.VMEM((dim, row_count), BF16),
            pltpu.SemaphoreType.DMA((2 + 3 * PARTS,)),
        ],
        compiler_params=PARAMS,
        name="gradients",
    )(*in_hbm(features, aggregated, cotangent, w_self, w_neigh))
    own = pl.pallas_call(
        kept_kernel,
        out_shape=pltpu.VMEM((dim, dim), F32),
        in_specs=[VMEM, VMEM, ANY],
        out_specs=VMEM,
        compiler_params=PARAMS,
        name="kept_sum",
    )(inputs, pre_grad, given)

    half = own + swap(given, "hst", 0).astype(F32)
    quarter = dim // 2
    low, high = half[:quarter], half[quarter:]
    kept, given = jnp.where(odd, high, low), jnp.where(odd, low, high).astype(BF16)
    kept = kept + swap(given, "dom", 0).astype(F32)

    neigh_grad, outgoing = pl.pallas_call(
        outgoing_kernel,
        out_shape=(struct((row_count, dim), BF16), struct((peers * cap, dim), BF16)),
        in_specs=[SMEM, VMEM, VMEM, VMEM, VMEM, ANY],
        out_specs=(VMEM, VMEM),
        compiler_params=PARAMS,
        name="outgoing",
    )(
        send_count,
        pre_grad,
        w_neigh,
        jnp.swapaxes(slot_source[0], 1, 2),
        jnp.swapaxes(slot_weight[0], 1, 2),
        given,
    )
    held = outgoing.reshape(1, peers * cap, dim)
    scale = 1.0 / math.sqrt(row_count * lax.axis_size("hst") * peers)
    for step, bit in enumerate(hop_bits(peers)):
        given = (kept if bit else kept * scale).astype(BF16)
        middle = held.shape[1] // 2
        stay, moved = held[:, :middle], held[:, middle:].reshape(-1, dim)
        arrived = swap(jnp.concatenate([given, moved], axis=0), "dom", bit)
        if step == 0:
            cross_out, stay = pl.pallas_call(
                stale_kernel,
                out_shape=(
                    struct((cross_source.shape[1], dim), BF16),
                    struct(stay.shape, stay.dtype),
                ),
                in_specs=[SMEM, SMEM, VMEM, VMEM, VMEM, VMEM, ANY],
                out_specs=(VMEM, ANY),
                input_output_aliases={6: 1},
                compiler_params=PARAMS,
                name="stale_rows",
            )(
                version,
                cross_count,
                stale_grad[0],
                w_neigh,
                cross_source[0].T,
                cross_weight[0].T,
                stay,
            )
        if step == 1:
            base, hit, stay = pl.pallas_call(
                local_kernel,
                out_shape=(
                    struct((blocks, 128, dim), F32),
                    struct((row_count, peers * cap + cross_rows.shape[1]), BF16),
                    struct(stay.shape, stay.dtype),
                ),
                in_specs=[SMEM, VMEM, VMEM, VMEM, VMEM, VMEM, VMEM, ANY],
                out_specs=(VMEM, VMEM, ANY),
                input_output_aliases={7: 2},
                compiler_params=PARAMS,
                name="local_term",
            )(
                tile_source,
                pre_grad,
                neigh_grad,
                w_self,
                tile_values[0],
                recv_rows[0],
                cross_rows,
                stay,
            )
        other = arrived[:quarter]
        kept = given.astype(F32) + other.astype(F32)
        held = jnp.stack([stay, arrived[quarter:].reshape(stay.shape)], axis=1)
        held = held.reshape(-1, middle, dim)
    early = swap(jnp.concatenate([given, cross_out], axis=0), "hst", 0)
    stale_in = early[quarter:]
    last = swap(other, "hst", 0)
    out_rows, sums = pl.pallas_call(
        finish_kernel,
        out_shape=(struct((row_count, dim), BF16), struct((2, dim, dim), BF16)),
        in_specs=[VMEM] * 7,
        out_specs=(ANY, ANY),
        scratch_shapes=[
            pltpu.VMEM((row_count, dim), BF16),
            pltpu.SemaphoreType.DMA((3 + pl.cdiv(blocks, OUT_BLOCKS),)),
        ],
        compiler_params=PARAMS,
        name="finish",
    )(
        base,
        held.reshape(peers * cap, dim),
        stale_in,
        hit,
        given,
        other,
        early[:quarter],
    )
    sums = pl.pallas_call(
        last_kernel,
        out_shape=struct((2, dim, dim), BF16),
        in_specs=[VMEM, ANY],
        out_specs=ANY,
        input_output_aliases={1: 0},
        scratch_shapes=[pltpu.SemaphoreType.DMA],
        compiler_params=PARAMS,
        name="weight_grads",
    )(last, sums)
    return (out_rows, sums)


def solution(mesh):
    rows = ("runs", "hst", "dom")
    specs = [P(rows)] * 17
    specs[3] = specs[4] = P()
    return jax.shard_map(
        body,
        mesh=mesh,
        in_specs=tuple(specs),
        out_specs=(P(rows), P("runs")),
        check_vma=False,
    )
```
